512 devices in a mesh: dp: 16 (over z_hi, y), mp: 32 (over z_lo, x, core).
Axes of the slice: x: 4, y: 4, z: 16 (z_hi: 4, z_lo: 4; z = z_hi * 4 + z_lo), core: 2. Of those that a mesh axis runs over, the one named last changes fastest.
Arguments:
- teacher_hidden: bfloat16 [224, 26624], P('dp', 'mp'), may hold values from -6 to 6
- teacher_down: bfloat16 [26624, 16384], P('mp', 'dp'), may hold values from -0.0390625 to 0.0390625
- scale_index: int32 [416], P('mp'), may hold values from 0 to 6
- distill_proj: bfloat16 [16384, 8192], P('dp', 'mp'), may hold values from -0.046875 to 0.046875
- assignment: int32 [224], replicated, may hold values from 0 to 223, each once
- student_input: bfloat16 [224, 8192], P('dp', 'mp'), may hold values from -6 to 6
- w_gate: bfloat16 [8192, 14336], P('mp', 'dp'), may hold values from -0.0625 to 0.0625
- w_up: bfloat16 [8192, 14336], P('mp', 'dp'), may hold values from -0.0625 to 0.0625
- w_down: bfloat16 [14336, 8192], P('dp', 'mp'), may hold values from -0.046875 to 0.046875
Outputs:
- grad_gate: bfloat16 [8192, 14336], P('mp', 'dp')
- grad_up: bfloat16 [8192, 14336], P('mp', 'dp')
- grad_down: bfloat16 [14336, 8192], P('dp', 'mp')
- input_grad: bfloat16 [224, 8192], P('dp', 'mp')
The draws below stay inside these ranges and needn't reach their ends.
All inputs are finite; a program needn't handle non-finite values. Where the reference program divides by a largest or mean magnitude, that divisor is 1e-20 or more.
Results may differ from the reference program's by a relative error of at most 0.008.
Values may be sent and summed in bfloat16 or wider, within the bound.
A program may use at most 64 MiB of HBM per device.

```python
import jax
import jax.numpy as jnp

DT = 16384
FT = 26624
DS = 8192
FS = 14336
GROUP = 64
TOKENS = 224


def place_ends(result, stream_key, least, top_value):
    index_at = [jax.random.randint(jax.random.fold_in(stream_key, axis), (), 0, length) for axis, length in enumerate(result.shape)]
    widest = result.shape.index(max(result.shape))
    neighbour = index_at[:widest] + [(index_at[widest] + 1) % result.shape[widest]] + index_at[widest + 1:]
    return result.at[tuple(index_at)].set(least).at[tuple(neighbour)].set(top_value)


def levels(stream_key, dims, pieces, low, largest):
    factor_of = 1.0
    for axis_at, parts in pieces:
        draws = jax.random.uniform(jax.random.fold_in(jax.random.fold_in(stream_key, 6), axis_at), (parts,), jnp.float32, low / len(pieces), largest / len(pieces))
        factor_of = factor_of * jnp.repeat(jnp.exp(draws), dims[axis_at] // parts).reshape((-1,) + (1,) * (len(dims) - 1 - axis_at))
    return factor_of


def noise(own_key, dims, width, bound, shards=(), dtype=jnp.bfloat16):
    factor_of = levels(own_key, dims, shards, -0.22, 0.18) if shards else 1.0
    array = jax.random.normal(own_key, dims, jnp.float32) * width * factor_of
    return jnp.minimum(jnp.maximum(array, -bound), bound).astype(dtype)


def setup_inputs(seed: int = 0) -> dict:
    streams_of = jax.random.split(jax.random.key(seed), 10)
    return {
        "teacher_hidden": noise(streams_of[0], (TOKENS, FT), 1.0, 6.0, ((0, 16), (1, 32))),
        "teacher_down": noise(streams_of[1], (FT, DT), FT ** -0.5, 0.0390625, ((0, 32), (1, 16))),
        "scale_index": place_ends(jax.random.randint(streams_of[2], (FT // GROUP,), 0, 7), jax.random.fold_in(streams_of[2], 1), 0, 6).astype(jnp.int32),
        "distill_proj": noise(streams_of[3], (DT, DS), DT ** -0.5, 0.046875, ((0, 16), (1, 32))),
        "assignment": jax.random.permutation(streams_of[4], TOKENS).astype(jnp.int32),
        "student_input": noise(streams_of[5], (TOKENS, DS), 1.0, 6.0, ((0, 16), (1, 32))),
        "w_gate": noise(streams_of[6], (DS, FS), DS ** -0.5, 0.0625, ((0, 32), (1, 16))),
        "w_up": noise(streams_of[7], (DS, FS), DS ** -0.5, 0.0625, ((0, 32), (1, 16))),
        "w_down": noise(streams_of[8], (FS, DS), FS ** -0.5, 0.046875, ((0, 16), (1, 32))),
    }


target_range = 4.0


def reference(teacher_hidden, teacher_down, scale_index, distill_proj, assignment, student_input, w_gate, w_up, w_down):
    scales = jnp.repeat(jnp.exp2(scale_index.astype(jnp.float32) - 3.0), GROUP)
    scaled = (teacher_hidden.astype(jnp.float32) * scales).astype(jnp.bfloat16)
    teacher_out = jnp.dot(scaled, teacher_down, preferred_element_type=jnp.float32).astype(jnp.bfloat16)
    amax = jnp.max(jnp.abs(teacher_out.astype(jnp.float32)))
    picked = jnp.take(teacher_out, assignment.astype(jnp.int32), axis=0)
    target = jnp.dot(picked, distill_proj, preferred_element_type=jnp.float32) * (target_range / amax)
    gate = jnp.dot(student_input, w_gate, preferred_element_type=jnp.float32)
    up = jnp.dot(student_input, w_up, preferred_element_type=jnp.float32)
    hidden = (jax.nn.silu(gate) * up).astype(jnp.bfloat16)
    student_out = jnp.dot(hidden, w_down, preferred_element_type=jnp.float32)
    out_grad = ((student_out - target) * 0.5).astype(jnp.bfloat16)
    grad_down = jnp.dot(hidden.T, out_grad, preferred_element_type=jnp.float32).astype(jnp.bfloat16)
    hidden_grad = jnp.dot(out_grad, w_down.T, preferred_element_type=jnp.float32)
    sig = jax.nn.sigmoid(gate)
    gate_grad = (hidden_grad * up * sig * (1.0 + gate * (1.0 - sig))).astype(jnp.bfloat16)
    up_grad = (hidden_grad * gate * sig).astype(jnp.bfloat16)
    grad_gate = jnp.dot(student_input.T, gate_grad, preferred_element_type=jnp.float32).astype(jnp.bfloat16)
    grad_up = jnp.dot(student_input.T, up_grad, preferred_element_type=jnp.float32).astype(jnp.bfloat16)
    input_grad = (jnp.dot(gate_grad, w_gate.T, preferred_element_type=jnp.float32)
                  + jnp.dot(up_grad, w_up.T, preferred_element_type=jnp.float32)).astype(jnp.bfloat16)
    return grad_gate, grad_up, grad_down, input_grad
```

```python
import functools

import jax
import jax.numpy as jnp
from jax import lax
from jax.experimental import pallas as pl
from jax.experimental.pallas import tpu as pltpu
from jax.sharding import PartitionSpec as P

MESH = pl.DeviceIdType.MESH
BF, F32 = jnp.bfloat16, jnp.float32
ROWS = 16
KS = (1, 3, 2)

RECV = {}
N_RECV = 0
for _name, _n in (
    ("Sz", 4), ("Sy", 16), ("Tz", 4), ("Ty", 16), ("Sc", 2), ("Tc", 1), ("Sx", 4), ("Tx", 4), ("Szl", 4), ("Tzl", 4),
    ("Hzl", 4), ("ABzl", 4), ("Hx", 4), ("Hc", 4), ("ABx", 4), ("ABc", 4), ("Tax", 4), ("Tac", 4),
    ("Mz", 4), ("My", 4), ("Mx", 4), ("Mc", 1), ("TPy", 4), ("SPy", 4), ("Oz", 4), ("Oy", 4),
    ("Gc", 1), ("Gx", 4), ("Gzl", 4), ("Gax", 4), ("Gac", 4), ("Iy", 4), ("Iz", 4),
):
    RECV[_name] = N_RECV
    N_RECV += _n
N_SEND = 150


def dot(a, b):
    return jnp.dot(a, b, preferred_element_type=F32)


def dot_nt(a, b):
    return lax.dot_general(a, b, (((1,), (1,)), ((), ())), preferred_element_type=F32)


def dot_tn(a, b):
    return lax.dot_general(a, b, (((0,), (0,)), ((), ())), preferred_element_type=F32)


def kernel(
    th, xin, perm, td_h, dp_h, wg_h, wu_h, wd_h,
    gg_o, gu_o, gd_o, ig_o,
    td, dpj, wg, wu, wd, TG, XG, XT,
    SCs, SCr, SOWN, SXs, SXr, SZf, SZs, SZr, HZ, ABZ, HID, AB,
    TCs, TCr, TOWN, TXs, TXr, TZ, TO, AM0, AMz, AMy, AMx, AMc,
    TPf, TPr, SPf, SPr, OZ, OG,
    GCs, GCr, GOWN, GXs, GXr, GZ, HG, GG, UG, IPf, IPs, IPr, IZf, IZs, IZr,
    send_sem, recv_sem, load_sem,
):
    d, m = lax.axis_index("dp"), lax.axis_index("mp")
    zh, y, zl, x, c = d // 4, d % 4, m // 8, (m // 2) % 4, m % 2
    oc = 1 - c

    def turn(v, k):
        return lax.rem(v + k, 4)

    def at(zh=zh, y=y, zl=zl, x=x, c=c):
        return (zh * 4 + y, zl * 8 + x * 2 + c)

    core = at(c=oc)
    x_dev = lambda v: at(x=v)
    y_dev = lambda v: at(y=v)
    zl_dev = lambda v: at(zl=v)
    zh_dev = lambda v: at(zh=v)

    sent = []

    def send(src, dst, dev, name, slot):
        copy = pltpu.make_async_remote_copy(
            src, dst, send_sem.at[len(sent)], recv_sem.at[RECV[name] + slot], device_id=dev, device_id_type=MESH
        )
        copy.start()
        sent.append(copy)

    def arrive(dst, name, slot):
        pltpu.make_async_remote_copy(
            dst, dst, send_sem.at[0], recv_sem.at[RECV[name] + slot], device_id=core, device_id_type=MESH
        ).wait_recv()

    barrier = pltpu.get_barrier_semaphore()
    partners = [core]
    for k in KS:
        partners += [x_dev(turn(x, k)), y_dev(turn(y, k)), zl_dev(turn(zl, k)), zh_dev(turn(zh, k))]
    for p in partners:
        pl.semaphore_signal(barrier, inc=1, device_id=p, device_id_type=MESH)
    loads = [
        pltpu.make_async_copy(a, b, load_sem.at[i])
        for i, (a, b) in enumerate(((wg_h, wg), (wu_h, wu), (td_h, td), (dp_h, dpj), (wd_h, wd)))
    ]
    for load in loads:
        load.start()
    XG[zh, y] = xin[...]
    TG[zh, y] = th[...]
    pl.semaphore_wait(barrier, len(partners))

    for buf, nz, ny in ((XG, "Sz", "Sy"), (TG, "Tz", "Ty")):
        own = buf.at[zh, y]
        for k in KS:
            send(own, own, zh_dev(turn(zh, k)), nz, zh)
        for k in KS:
            send(own, own, y_dev(turn(y, k)), ny, zh * 4 + y)
    for buf, nz, ny in ((XG, "Sz", "Sy"), (TG, "Tz", "Ty")):
        for k in KS:
            z = turn(zh, k)
            arrive(buf.at[z, y], nz, z)
            for j in KS:
                send(buf.at[z, y], buf.at[z, y], y_dev(turn(y, j)), ny, z * 4 + y)

    for j in KS:
        for z in range(4):
            arrive(XG.at[z, turn(y, j)], "Sy", z * 4 + turn(y, j))
    loads[0].wait()
    loads[1].wait()
    half = XG[pl.ds(2 * oc, 2)].reshape(128, -1)
    for a, w in enumerate((wg, wu)):
        SCs[a] = dot(half, w[...]).reshape(SCs.shape[1:])
        send(SCs.at[a], SCr.at[a], core, "Sc", a)
    half = XG[pl.ds(2 * c, 2)].reshape(128, -1)
    for a, w in enumerate((wg, wu)):
        SOWN[a] = dot(half, w[...]).reshape(SOWN.shape[1:])

    for j in KS:
        for z in range(4):
            arrive(TG.at[z, turn(y, j)], "Ty", z * 4 + turn(y, j))
    loads[2].wait()
    everything = TG[...].reshape(16 * ROWS, -1)
    picked = dot(perm[pl.ds(oc, 1)].reshape(128, -1), everything).astype(BF)
    TCs[...] = dot(picked, td[...]).reshape(TCs.shape)
    send(TCs, TCr, core, "Tc", 0)
    picked = dot(perm[pl.ds(c, 1)].reshape(128, -1), everything).astype(BF)
    TOWN[...] = dot(picked, td[...]).reshape(TOWN.shape)

    for a in range(2):
        arrive(SCr.at[a], "Sc", a)
    for k in KS:
        v = turn(x, k)
        for a in range(2):
            SXs[v, a] = (SOWN[a, v] + SCr[a, v]).astype(BF)
        send(SXs.at[v], SXr.at[x], x_dev(v), "Sx", x)
    arrive(TCr, "Tc", 0)
    for k in KS:
        v = turn(x, k)
        TXs[v] = (TOWN[v] + TCr[v]).astype(BF)
        send(TXs.at[v], TXr.at[x], x_dev(v), "Tx", x)
    XT[...] = XG[...].reshape(16 * ROWS, -1).T

    fs = SOWN.shape[-1]
    shift = fs - 512
    for k in KS:
        arrive(SXr.at[turn(x, k)], "Sx", turn(x, k))
    for a in range(2):
        total = SOWN[a, x] + SCr[a, x]
        for k in KS:
            total = total + SXr[turn(x, k), a].astype(F32)
        for w in range(4):
            r, h = w % 2, w // 2
            part = total[r * 16 : r * 16 + 16, h * shift : h * shift + 512]
            SZf[w, a] = part
            SZs[w, a] = part.astype(BF)
    for k in KS:
        v = turn(zl, k)
        send(SZs.at[v], SZr.at[zl], zl_dev(v), "Szl", zl)
    for k in KS:
        arrive(TXr.at[turn(x, k)], "Tx", turn(x, k))
    total = TOWN[x] + TCr[x]
    for k in KS:
        total = total + TXr[turn(x, k)].astype(F32)
    TZ[zl] = total.astype(BF)
    for k in KS:
        send(TZ.at[zl], TZ.at[zl], zl_dev(turn(zl, k)), "Tzl", zl)

    for k in KS:
        arrive(SZr.at[turn(zl, k)], "Szl", turn(zl, k))
    pre = []
    for a in range(2):
        total = SZf[zl, a]
        for k in KS:
            total = total + SZr[turn(zl, k), a].astype(F32)
        pre.append(total)
    gate, up = pre
    sig = jax.nn.sigmoid(gate)
    HZ[zl] = (gate * sig * up).astype(BF)
    for k in KS:
        send(HZ.at[zl], HZ.at[zl], zl_dev(turn(zl, k)), "Hzl", zl)
    ABZ[zl, 0] = (up * sig * (1.0 + gate * (1.0 - sig))).astype(BF)
    ABZ[zl, 1] = (gate * sig).astype(BF)
    for k in KS:
        send(ABZ.at[zl], ABZ.at[zl], zl_dev(turn(zl, k)), "ABzl", zl)

    for k in KS:
        arrive(TZ.at[turn(zl, k)], "Tzl", turn(zl, k))
    total = TZ[0].astype(F32)
    for w in range(1, 4):
        total = total + TZ[w].astype(F32)
    teacher = total.astype(BF)
    TO[c, x] = teacher
    for k in KS:
        send(TO.at[c, x], TO.at[c, x], x_dev(turn(x, k)), "Tax", x)
    send(TO.at[c, x], TO.at[c, x], core, "Tac", x)
    AM0[...] = jnp.full(AM0.shape, jnp.max(jnp.abs(teacher.astype(F32))), F32)
    for k in KS:
        send(AM0, AMz.at[zh], zh_dev(turn(zh, k)), "Mz", zh)

    for k in KS:
        arrive(HZ.at[turn(zl, k)], "Hzl", turn(zl, k))
    for r in range(2):
        HID[c, x, r, :, 0:512] = HZ[r]
        HID[c, x, r, :, 512:fs] = HZ[2 + r][:, 512 - shift :]
    for k in KS:
        send(HID.at[c, x], HID.at[c, x], x_dev(turn(x, k)), "Hx", x)
    send(HID.at[c, x], HID.at[c, x], core, "Hc", x)

    for k in KS:
        v = turn(x, k)
        arrive(TO.at[c, v], "Tax", v)
        send(TO.at[c, v], TO.at[c, v], core, "Tac", v)
    for k in KS:
        v = turn(x, k)
        arrive(HID.at[c, v], "Hx", v)
        send(HID.at[c, v], HID.at[c, v], core, "Hc", v)
    biggest = AM0[...]
    for k in KS:
        arrive(AMz.at[turn(zh, k)], "Mz", turn(zh, k))
        biggest = jnp.maximum(biggest, AMz[turn(zh, k)])
    AMy[y] = biggest
    for k in KS:
        send(AMy.at[y], AMy.at[y], y_dev(turn(y, k)), "My", y)

    loads[3].wait()
    for w in range(4):
        arrive(TO.at[oc, w], "Tac", w)
    part = dot(TO[...].reshape(16 * ROWS, -1), dpj[...]).reshape(TPf.shape)
    TPf[...] = part
    for k in KS:
        v = turn(y, k)
        send(TPf.at[:, v], TPr.at[y], y_dev(v), "TPy", y)
    loads[4].wait()
    for w in range(4):
        arrive(HID.at[oc, w], "Hc", w)
    part = dot(HID[...].reshape(16 * ROWS, -1), wd[...]).reshape(SPf.shape)
    SPf[...] = part
    for k in KS:
        v = turn(y, k)
        send(SPf.at[:, v], SPr.at[y], y_dev(v), "SPy", y)

    for k in KS:
        arrive(AMy.at[turn(y, k)], "My", turn(y, k))
    AMx[x] = jnp.maximum(jnp.maximum(AMy[0], AMy[1]), jnp.maximum(AMy[2], AMy[3]))
    for k in KS:
        send(AMx.at[x], AMx.at[x], x_dev(turn(x, k)), "Mx", x)
    for k in KS:
        arrive(ABZ.at[turn(zl, k)], "ABzl", turn(zl, k))
    for a in range(2):
        for r in range(2):
            AB[c, x, a, r, :, 0:512] = ABZ[r, a]
            AB[c, x, a, r, :, 512:fs] = ABZ[2 + r, a][:, 512 - shift :]
    for k in KS:
        arrive(AMx.at[turn(x, k)], "Mx", turn(x, k))
    biggest = jnp.maximum(jnp.maximum(AMx[0], AMx[1]), jnp.maximum(AMx[2], AMx[3]))
    AM0c = AMc.at[0]
    AM0c[...] = biggest
    send(AMc.at[0], AMc.at[1], core, "Mc", 0)
    for k in KS:
        send(AB.at[c, x], AB.at[c, x], x_dev(turn(x, k)), "ABx", x)
    send(AB.at[c, x], AB.at[c, x], core, "ABc", x)

    for k in KS:
        arrive(TPr.at[turn(y, k)], "TPy", turn(y, k))
        arrive(SPr.at[turn(y, k)], "SPy", turn(y, k))
    arrive(AMc.at[1], "Mc", 0)
    scale = (4.0 / jnp.maximum(biggest, AMc[1]))[0:1, 0:1]
    for z in range(4):
        target, student = TPf[z, y], SPf[z, y]
        for k in KS:
            target = target + TPr[turn(y, k), z]
            student = student + SPr[turn(y, k), z]
        OZ[zh, z] = ((student - target * scale) * 0.5).astype(BF)
    for k in KS:
        send(OZ.at[zh], OZ.at[zh], zh_dev(turn(zh, k)), "Oz", zh)
    for k in KS:
        v = turn(x, k)
        arrive(AB.at[c, v], "ABx", v)
        send(AB.at[c, v], AB.at[c, v], core, "ABc", v)
    for k in KS:
        arrive(OZ.at[turn(zh, k)], "Oz", turn(zh, k))
    for z in range(4):
        total = OZ[0, z].astype(F32)
        for w in range(1, 4):
            total = total + OZ[w, z].astype(F32)
        OG[z, y] = total.astype(BF)
    for k in KS:
        send(OG.at[:, y], OG.at[:, y], y_dev(turn(y, k)), "Oy", y)
    for k in KS:
        arrive(OG.at[:, turn(y, k)], "Oy", turn(y, k))

    GCs[...] = dot_nt(OG[pl.ds(2 * oc, 2)].reshape(128, -1), wd[...]).reshape(GCs.shape)
    send(GCs, GCr, core, "Gc", 0)
    GOWN[...] = dot_nt(OG[pl.ds(2 * c, 2)].reshape(128, -1), wd[...]).reshape(GOWN.shape)
    arrive(GCr, "Gc", 0)
    for k in KS:
        v = turn(x, k)
        GXs[v] = (GOWN[v] + GCr[v]).astype(BF)
        send(GXs.at[v], GXr.at[x], x_dev(v), "Gx", x)
    gd_o[...] = dot_tn(HID[...].reshape(16 * ROWS, -1), OG[...].reshape(16 * ROWS, -1)).astype(BF)
    for k in KS:
        arrive(GXr.at[turn(x, k)], "Gx", turn(x, k))
    total = GOWN[x] + GCr[x]
    for k in KS:
        total = total + GXr[turn(x, k)].astype(F32)
    GZ[zl] = total.astype(BF)
    for k in KS:
        send(GZ.at[zl], GZ.at[zl], zl_dev(turn(zl, k)), "Gzl", zl)
    for w in range(4):
        arrive(AB.at[oc, w], "ABc", w)
    for k in KS:
        arrive(GZ.at[turn(zl, k)], "Gzl", turn(zl, k))
    total = GZ[0].astype(F32)
    for w in range(1, 4):
        total = total + GZ[w].astype(F32)
    HG[c, x] = total.astype(BF)
    for k in KS:
        send(HG.at[c, x], HG.at[c, x], x_dev(turn(x, k)), "Gax", x)
    send(HG.at[c, x], HG.at[c, x], core, "Gac", x)
    for k in KS:
        v = turn(x, k)
        arrive(HG.at[c, v], "Gax", v)
        send(HG.at[c, v], HG.at[c, v], core, "Gac", v)
    for w in range(4):
        arrive(HG.at[oc, w], "Gac", w)
    for cc in range(2):
        for v in range(4):
            g = HG[cc, v].astype(F32)
            GG[cc, v] = (g * AB[cc, v, 0].reshape(32, fs).astype(F32)).astype(BF)
            UG[cc, v] = (g * AB[cc, v, 1].reshape(32, fs).astype(F32)).astype(BF)

    gates, ups = GG[...].reshape(16 * ROWS, -1), UG[...].reshape(16 * ROWS, -1)
    part = (dot_nt(gates, wg[...]) + dot_nt(ups, wu[...])).reshape(IPf.shape)
    IPf[...] = part
    IPs[...] = part.astype(BF)
    for k in KS:
        v = turn(y, k)
        send(IPs.at[:, v], IPr.at[y], y_dev(v), "Iy", y)
    gg_o[...] = dot(XT[...], gates).astype(BF)
    for k in KS:
        arrive(IPr.at[turn(y, k)], "Iy", turn(y, k))
    for z in range(4):
        total = IPf[z, y]
        for k in KS:
            total = total + IPr[turn(y, k), z].astype(F32)
        IZf[z] = total
        IZs[z] = total.astype(BF)
    for k in KS:
        v = turn(zh, k)
        send(IZs.at[v], IZr.at[zh], zh_dev(v), "Iz", zh)
    gu_o[...] = dot(XT[...], ups).astype(BF)
    for k in KS:
        arrive(IZr.at[turn(zh, k)], "Iz", turn(zh, k))
    total = IZf[zh]
    for k in KS:
        total = total + IZr[turn(zh, k)].astype(F32)
    ig_o[...] = total.astype(BF)
    for copy in sent:
        copy.wait_send()


def body(
    teacher_hidden,
    teacher_down,
    scale_index,
    distill_proj,
    assignment,
    student_input,
    w_gate,
    w_up,
    w_down,
):
    tokens, ft = teacher_hidden.shape
    dt, ds = distill_proj.shape
    fs = w_gate.shape[1]
    scales = jnp.repeat(jnp.exp2(scale_index.astype(F32) - 3.0), ft // scale_index.shape[0])
    pad = ((0, ROWS - tokens), (0, 0))
    th = jnp.pad((teacher_hidden.astype(F32) * scales).astype(BF), pad)
    xin = jnp.pad(student_input, pad)
    place = (assignment // tokens) * ROWS + assignment % tokens
    place = jnp.pad(place.reshape(-1, tokens), ((0, 0), (0, ROWS - tokens)), constant_values=-1)
    perm = (place.reshape(2, 128, 1) == jnp.arange(16 * ROWS, dtype=jnp.int32)).astype(BF)

    def v(shape, dtype=BF):
        return pltpu.VMEM(shape, dtype)

    dp4 = (4, 4, ROWS)
    scratch = [
        v((ft, dt)), v((dt, ds)), v((ds, fs)), v((ds, fs)), v((fs, ds)), v(dp4 + (ft,)), v(dp4 + (ds,)), v((ds, 16 * ROWS)),
        v((2, 4, 32, fs), F32), v((2, 4, 32, fs), F32), v((2, 4, 32, fs), F32), v((4, 2, 32, fs)), v((4, 2, 32, fs)),
        v((4, 2, 16, 512), F32), v((4, 2, 16, 512)), v((4, 2, 16, 512)), v((4, 16, 512)), v((4, 2, 16, 512)),
        v((2, 4, 2, 16, fs)), v((2, 4, 2, 2, 16, fs)),
        v((4, 32, dt), F32), v((4, 32, dt), F32), v((4, 32, dt), F32), v((4, 32, dt)), v((4, 32, dt)), v((4, 32, dt)), v((2, 4, 32, dt)),
        v((8, 128), F32), v((4, 8, 128), F32), v((4, 8, 128), F32), v((4, 8, 128), F32), v((2, 8, 128), F32),
        v(dp4 + (ds,), F32), v(dp4 + (ds,), F32), v(dp4 + (ds,), F32), v(dp4 + (ds,), F32),
        v(dp4 + (ds,)), v(dp4 + (ds,)),
        v((4, 32, fs), F32), v((4, 32, fs), F32), v((4, 32, fs), F32), v((4, 32, fs)), v((4, 32, fs)), v((4, 32, fs)),
        v((2, 4, 32, fs)), v((2, 4, 32, fs)), v((2, 4, 32, fs)),
        v(dp4 + (ds,), F32), v(dp4 + (ds,)), v(dp4 + (ds,)), v((4, ROWS, ds), F32), v((4, ROWS, ds)), v((4, ROWS, ds)),
        pltpu.SemaphoreType.DMA((N_SEND,)), pltpu.SemaphoreType.DMA((N_RECV,)), pltpu.SemaphoreType.DMA((5,)),
    ]
    vm, hbm = pl.BlockSpec(memory_space=pltpu.VMEM), pl.BlockSpec(memory_space=pl.ANY)
    sds = jax.ShapeDtypeStruct
    grad_gate, grad_up, grad_down, input_grad = pl.pallas_call(
        kernel,
        out_shape=(sds((ds, fs), BF), sds((ds, fs), BF), sds((fs, ds), BF), sds((ROWS, ds), BF)),
        in_specs=[vm] * 3 + [hbm] * 5,
        out_specs=(vm,) * 4,
        scratch_shapes=scratch,
        compiler_params=pltpu.CompilerParams(collective_id=0, has_side_effects=True, vmem_limit_bytes=56 << 20),
        name="distill_step",
    )(th, xin, perm, teacher_down, distill_proj, w_gate, w_up, w_down)
    return grad_gate, grad_up, grad_down, input_grad[:tokens]


def solution(mesh):
    placed = (
        P("dp", "mp"),
        P("mp", "dp"),
        P("mp"),
        P("dp", "mp"),
        P(),
        P("dp", "mp"),
        P("mp", "dp"),
        P("mp", "dp"),
        P("dp", "mp"),
    )
    return jax.shard_map(
        body,
        mesh=mesh,
        in_specs=placed,
        out_specs=(P("mp", "dp"), P("mp", "dp"), P("dp", "mp"), P("dp", "mp")),
        check_vma=False,
    )
```

```python
import functools

import jax
import jax.numpy as jnp
from jax import lax
from jax.experimental import pallas as pl
from jax.experimental.pallas import tpu as pltpu
from jax.sharding import PartitionSpec as P

MESH = pl.DeviceIdType.MESH
BF, F32 = jnp.bfloat16, jnp.float32
ROWS = 16
KS = (2, 1, 3)

RECV = {}
N_RECV = 0
for _name, _n in (
    ("Sz", 4), ("Sy", 16), ("Tz", 4), ("Ty", 16), ("Sc", 2), ("Tc", 2), ("Sx", 8), ("Tx", 8), ("Szl", 8), ("Tzl", 8),
    ("Hzl", 4), ("ABzl", 4), ("Hx", 4), ("Hc", 4), ("ABx", 4), ("ABc", 4), ("Tax", 8), ("Tac", 8),
    ("Md", 16), ("Mc", 8), ("TPy", 4), ("SPy", 4), ("Oz", 4), ("Oy", 4),
    ("Gc", 2), ("Gx", 8), ("Gzl", 8), ("Gax", 8), ("Gac", 8), ("Iy", 4), ("Iz", 4),
):
    RECV[_name] = N_RECV
    N_RECV += _n
N_SEND = 170


def dot(a, b):
    return jnp.dot(a, b, preferred_element_type=F32)


def dot_nt(a, b):
    return lax.dot_general(a, b, (((1,), (1,)), ((), ())), preferred_element_type=F32)


def dot_tn(a, b):
    return lax.dot_general(a, b, (((0,), (0,)), ((), ())), preferred_element_type=F32)


def kernel(
    index, assign, th, xin, td_h, dp_h, wg_h, wu_h, wd_h,
    gg_o, gu_o, gd_o, ig_o,
    td, dpj, wg, wu, wd, perm, TG, XG, XT,
    SCs, SCr, SOWN, SXs, SXr, SZf, SZs, SZr, HZ, ABZ, HID, AB,
    TCs, TCr, TOWN, TXs, TXr, TZ, TO, AMd, AMc,
    TPf, TPr, SPf, SPr, OZ, OG,
    GCs, GCr, GOWN, GXs, GXr, GZ, HG, GG, UG, IPf, IPs, IPr, IZf, IZs, IZr,
    send_sem, recv_sem, load_sem,
):
    d, m = lax.axis_index("dp"), lax.axis_index("mp")
    zh, y, zl, x, c = d // 4, d % 4, m // 8, (m // 2) % 4, m % 2
    oc = 1 - c

    def turn(v, k):
        return lax.rem(v + k, 4)

    def at(zh=zh, y=y, zl=zl, x=x, c=c):
        return (zh * 4 + y, zl * 8 + x * 2 + c)

    core = at(c=oc)
    x_dev = lambda v: at(x=v)
    y_dev = lambda v: at(y=v)
    zl_dev = lambda v: at(zl=v)
    zh_dev = lambda v: at(zh=v)

    sent = []

    def send(src, dst, dev, name, slot):
        copy = pltpu.make_async_remote_copy(
            src, dst, send_sem.at[len(sent)], recv_sem.at[RECV[name] + slot], device_id=dev, device_id_type=MESH
        )
        copy.start()
        sent.append(copy)

    def arrive(dst, name, slot):
        pltpu.make_async_remote_copy(
            dst, dst, send_sem.at[0], recv_sem.at[RECV[name] + slot], device_id=core, device_id_type=MESH
        ).wait_recv()

    def scatter_x(own, other, out, into, n_core, n_x, r):
        arrive(other.at[:, r], n_core, r)
        for k in KS:
            v = turn(x, k)
            out[v, r] = (own[v, r] + other[v, r]).astype(BF)
            send(out.at[v, r], into.at[x, r], x_dev(v), n_x, x * 2 + r)

    def share_zl(own, other, into, shares, n_x, n_zl, r):
        total = own[x, r] + other[x, r]
        for k in KS:
            arrive(into.at[turn(x, k), r], n_x, turn(x, k) * 2 + r)
        for k in KS:
            total = total + into[turn(x, k), r].astype(F32)
        shares[zl, r] = total.astype(BF)
        for k in KS:
            send(shares.at[zl, r], shares.at[zl, r], zl_dev(turn(zl, k)), n_zl, zl * 2 + r)

    def gather_x(shares, result, n_zl, n_x, n_core, r):
        for k in KS:
            arrive(shares.at[turn(zl, k), r], n_zl, turn(zl, k) * 2 + r)
        total = shares[0, r].astype(F32)
        for w in range(1, 4):
            total = total + shares[w, r].astype(F32)
        result[c, x, r] = total.astype(BF)
        mine = result.at[c, x, r]
        for k in KS:
            send(mine, mine, x_dev(turn(x, k)), n_x, x * 2 + r)
        send(mine, mine, core, n_core, x * 2 + r)

    def pass_on(result, n_x, n_core, r):
        for k in KS:
            v = turn(x, k)
            arrive(result.at[c, v, r], n_x, v * 2 + r)
            send(result.at[c, v, r], result.at[c, v, r], core, n_core, v * 2 + r)

    barrier = pltpu.get_barrier_semaphore()
    partners = [core]
    for k in KS:
        partners += [x_dev(turn(x, k)), at(x=turn(x, k), c=oc), zl_dev(turn(zl, k))]
    dp_group = [at(zh=turn(zh, i), y=turn(y, j)) for i in KS + (0,) for j in KS + (0,)][:-1]
    pairs = [at(x=turn(x, k), c=b) for k in KS for b in (oc, c)] + [core]
    partners += dp_group
    for p in partners:
        pl.semaphore_signal(barrier, inc=1, device_id=p, device_id_type=MESH)
    loads = [
        pltpu.make_async_copy(a, b, load_sem.at[i])
        for i, (a, b) in enumerate(((wg_h, wg), (wu_h, wu), (td_h, td), (dp_h, dpj), (wd_h, wd)))
    ]
    for load in loads:
        load.start()
    tokens, ft = th.shape
    groups = index.shape[0]

    def padded(rows):
        return jnp.concatenate([rows, jnp.zeros((ROWS - tokens, rows.shape[1]), F32)], axis=0).astype(BF)

    XG[zh, y] = padded(xin[...].astype(F32))
    group = lax.broadcasted_iota(jnp.int32, (1, ft), 1) // (ft // groups)
    level = jnp.zeros((1, ft), jnp.int32)
    for i in range(groups):
        level = jnp.where(group == i, index[i], level)
    scales = jnp.full((1, ft), 0.125, F32)
    for i in range(1, 7):
        scales = jnp.where(level == i, 0.125 * 2**i, scales)
    TG[zh, y] = padded(th[...].astype(F32) * scales)

    def place(block, carry):
        row = lax.broadcasted_iota(jnp.int32, (ROWS, 16 * ROWS), 0)
        column = lax.broadcasted_iota(jnp.int32, (ROWS, 16 * ROWS), 1)
        source = jnp.full((ROWS, 16 * ROWS), -1, jnp.int32)
        for i in range(tokens):
            a = assign[block * tokens + i]
            source = jnp.where(row == i, lax.div(a, tokens) * ROWS + lax.rem(a, tokens), source)
        perm[block] = jnp.where(source == column, 1.0, 0.0).astype(BF)
        return carry

    lax.fori_loop(0, 16, place, 0)
    pl.semaphore_wait(barrier, len(partners))

    for buf, nz, ny in ((XG, "Sz", "Sy"), (TG, "Tz", "Ty")):
        own = buf.at[zh, y]
        for k in KS:
            send(own, own, zh_dev(turn(zh, k)), nz, zh)
        for k in KS:
            send(own, own, y_dev(turn(y, k)), ny, zh * 4 + y)
    for buf, nz, ny in ((XG, "Sz", "Sy"), (TG, "Tz", "Ty")):
        for k in KS:
            z = turn(zh, k)
            arrive(buf.at[z, y], nz, z)
            for j in KS:
                send(buf.at[z, y], buf.at[z, y], y_dev(turn(y, j)), ny, z * 4 + y)

    for j in KS:
        for z in range(4):
            arrive(XG.at[z, turn(y, j)], "Sy", z * 4 + turn(y, j))
    loads[0].wait()
    loads[1].wait()
    half = XG[pl.ds(2 * oc, 2)].reshape(128, -1)
    for a, w in enumerate((wg, wu)):
        SCs[a] = dot(half, w[...]).reshape(SCs.shape[1:])
        send(SCs.at[a], SCr.at[a], core, "Sc", a)
    half = XG[pl.ds(2 * c, 2)].reshape(128, -1)
    for a, w in enumerate((wg, wu)):
        SOWN[a] = dot(half, w[...]).reshape(SOWN.shape[1:])

    for j in KS:
        for z in range(4):
            arrive(TG.at[z, turn(y, j)], "Ty", z * 4 + turn(y, j))
    loads[2].wait()
    everything = TG[...].reshape(16 * ROWS, -1)
    picked = dot(perm[pl.ds(8 * oc, 8)].reshape(128, -1), everything).astype(BF)
    TCs[...] = dot(picked, td[...]).reshape(TCs.shape)
    for r in range(2):
        send(TCs.at[:, r], TCr.at[:, r], core, "Tc", r)
    picked = dot(perm[pl.ds(8 * c, 8)].reshape(128, -1), everything).astype(BF)
    TOWN[...] = dot(picked, td[...]).reshape(TOWN.shape)

    for a in range(2):
        arrive(SCr.at[a], "Sc", a)
        for k in KS:
            v = turn(x, k)
            SXs[v, a] = (SOWN[a, v] + SCr[a, v]).astype(BF)
            send(SXs.at[v, a], SXr.at[x, a], x_dev(v), "Sx", x * 2 + a)
    for r in range(2):
        scatter_x(TOWN, TCr, TXs, TXr, "Tc", "Tx", r)
    XT[...] = XG[...].reshape(16 * ROWS, -1).T

    fs = SOWN.shape[-1]
    shift = fs - 512
    for a in range(2):
        for k in KS:
            arrive(SXr.at[turn(x, k), a], "Sx", turn(x, k) * 2 + a)
        total = SOWN[a, x] + SCr[a, x]
        for k in KS:
            total = total + SXr[turn(x, k), a].astype(F32)
        for w in range(4):
            r, h = w % 2, w // 2
            part = total[r * 16 : r * 16 + 16, h * shift : h * shift + 512]
            SZf[w, a] = part
            SZs[w, a] = part.astype(BF)
        for k in KS:
            v = turn(zl, k)
            send(SZs.at[v, a], SZr.at[zl, a], zl_dev(v), "Szl", zl * 2 + a)
    for r in range(2):
        share_zl(TOWN, TCr, TXr, TZ, "Tx", "Tzl", r)

    pre = []
    for a in range(2):
        for k in KS:
            arrive(SZr.at[turn(zl, k), a], "Szl", turn(zl, k) * 2 + a)
        total = SZf[zl, a]
        for k in KS:
            total = total + SZr[turn(zl, k), a].astype(F32)
        pre.append(total)
    gate, up = pre
    sig = jax.nn.sigmoid(gate)
    HZ[zl] = (gate * sig * up).astype(BF)
    for k in KS:
        send(HZ.at[zl], HZ.at[zl], zl_dev(turn(zl, k)), "Hzl", zl)
    ABZ[zl, 0] = (up * sig * (1.0 + gate * (1.0 - sig))).astype(BF)
    ABZ[zl, 1] = (gate * sig).astype(BF)
    for k in KS:
        send(ABZ.at[zl], ABZ.at[zl], zl_dev(turn(zl, k)), "ABzl", zl)

    for r in range(2):
        gather_x(TZ, TO, "Tzl", "Tax", "Tac", r)
    AMd[zh, y] = jnp.full((8, 128), jnp.max(jnp.abs(TO[c, x].astype(F32))), F32)
    for p in dp_group:
        send(AMd.at[zh, y], AMd.at[zh, y], p, "Md", zh * 4 + y)

    for k in KS:
        arrive(HZ.at[turn(zl, k)], "Hzl", turn(zl, k))
    for r in range(2):
        HID[c, x, r, :, 0:512] = HZ[r]
        HID[c, x, r, :, 512:fs] = HZ[2 + r][:, 512 - shift :]
    for k in KS:
        send(HID.at[c, x], HID.at[c, x], x_dev(turn(x, k)), "Hx", x)
    send(HID.at[c, x], HID.at[c, x], core, "Hc", x)

    for r in range(2):
        pass_on(TO, "Tax", "Tac", r)
    for k in KS:
        v = turn(x, k)
        arrive(HID.at[c, v], "Hx", v)
        send(HID.at[c, v], HID.at[c, v], core, "Hc", v)

    loads[3].wait()
    for w in range(8):
        arrive(TO.at[oc, w // 2, w % 2], "Tac", w)
    part = dot(TO[...].reshape(16 * ROWS, -1), dpj[...]).reshape(TPf.shape)
    TPf[...] = part
    for k in KS:
        v = turn(y, k)
        send(TPf.at[:, v], TPr.at[y], y_dev(v), "TPy", y)
    loads[4].wait()
    for w in range(4):
        arrive(HID.at[oc, w], "Hc", w)
    part = dot(HID[...].reshape(16 * ROWS, -1), wd[...]).reshape(SPf.shape)
    SPf[...] = part
    for k in KS:
        v = turn(y, k)
        send(SPf.at[:, v], SPr.at[y], y_dev(v), "SPy", y)

    for i in KS + (0,):
        for j in KS + (0,):
            if i or j:
                arrive(AMd.at[turn(zh, i), turn(y, j)], "Md", turn(zh, i) * 4 + turn(y, j))
    AMc[x, c] = jnp.max(AMd[...].reshape(16, 8, 128), axis=0)
    for p in pairs:
        send(AMc.at[x, c], AMc.at[x, c], p, "Mc", x * 2 + c)
    for k in KS:
        arrive(ABZ.at[turn(zl, k)], "ABzl", turn(zl, k))
    for a in range(2):
        for r in range(2):
            AB[c, x, a, r, :, 0:512] = ABZ[r, a]
            AB[c, x, a, r, :, 512:fs] = ABZ[2 + r, a][:, 512 - shift :]
    for k in KS:
        send(AB.at[c, x], AB.at[c, x], x_dev(turn(x, k)), "ABx", x)
    send(AB.at[c, x], AB.at[c, x], core, "ABc", x)

    for k in KS:
        arrive(TPr.at[turn(y, k)], "TPy", turn(y, k))
        arrive(SPr.at[turn(y, k)], "SPy", turn(y, k))
    for k in KS:
        for b in range(2):
            arrive(AMc.at[turn(x, k), b], "Mc", turn(x, k) * 2 + b)
    arrive(AMc.at[x, oc], "Mc", x * 2 + oc)
    scale = (4.0 / jnp.max(AMc[...].reshape(8, 8, 128), axis=0))[0:1, 0:1]
    for z in range(4):
        target, student = TPf[z, y], SPf[z, y]
        for k in KS:
            target = target + TPr[turn(y, k), z]
            student = student + SPr[turn(y, k), z]
        OZ[zh, z] = ((student - target * scale) * 0.5).astype(BF)
    for k in KS:
        send(OZ.at[zh], OZ.at[zh], zh_dev(turn(zh, k)), "Oz", zh)
    for k in KS:
        v = turn(x, k)
        arrive(AB.at[c, v], "ABx", v)
        send(AB.at[c, v], AB.at[c, v], core, "ABc", v)
    for k in KS:
        arrive(OZ.at[turn(zh, k)], "Oz", turn(zh, k))
    for z in range(4):
        total = OZ[0, z].astype(F32)
        for w in range(1, 4):
            total = total + OZ[w, z].astype(F32)
        OG[z, y] = total.astype(BF)
    for k in KS:
        send(OG.at[:, y], OG.at[:, y], y_dev(turn(y, k)), "Oy", y)
    for k in KS:
        arrive(OG.at[:, turn(y, k)], "Oy", turn(y, k))

    GCs[...] = dot_nt(OG[pl.ds(2 * oc, 2)].reshape(128, -1), wd[...]).reshape(GCs.shape)
    for r in range(2):
        send(GCs.at[:, r], GCr.at[:, r], core, "Gc", r)
    GOWN[...] = dot_nt(OG[pl.ds(2 * c, 2)].reshape(128, -1), wd[...]).reshape(GOWN.shape)
    for r in range(2):
        scatter_x(GOWN, GCr, GXs, GXr, "Gc", "Gx", r)
    gd_o[...] = dot_tn(HID[...].reshape(16 * ROWS, -1), OG[...].reshape(16 * ROWS, -1)).astype(BF)
    for r in range(2):
        share_zl(GOWN, GCr, GXr, GZ, "Gx", "Gzl", r)
    for w in range(4):
        arrive(AB.at[oc, w], "ABc", w)
    for r in range(2):
        gather_x(GZ, HG, "Gzl", "Gax", "Gac", r)
    for r in range(2):
        pass_on(HG, "Gax", "Gac", r)
    for w in range(8):
        arrive(HG.at[oc, w // 2, w % 2], "Gac", w)
    for cc in range(2):
        for v in range(4):
            g = HG[cc, v].astype(F32)
            GG[cc, v] = (g * AB[cc, v, 0].astype(F32)).astype(BF)
            UG[cc, v] = (g * AB[cc, v, 1].astype(F32)).astype(BF)

    gates, ups = GG[...].reshape(16 * ROWS, -1), UG[...].reshape(16 * ROWS, -1)
    part = (dot_nt(gates, wg[...]) + dot_nt(ups, wu[...])).reshape(IPf.shape)
    IPf[...] = part
    IPs[...] = part.astype(BF)
    for k in KS:
        v = turn(y, k)
        send(IPs.at[:, v], IPr.at[y], y_dev(v), "Iy", y)
    gg_o[...] = dot(XT[...], gates).astype(BF)
    for k in KS:
        arrive(IPr.at[turn(y, k)], "Iy", turn(y, k))
    for z in range(4):
        total = IPf[z, y]
        for k in KS:
            total = total + IPr[turn(y, k), z].astype(F32)
        IZf[z] = total
        IZs[z] = total.astype(BF)
    for k in KS:
        v = turn(zh, k)
        send(IZs.at[v], IZr.at[zh], zh_dev(v), "Iz", zh)
    gu_o[...] = dot(XT[...], ups).astype(BF)
    for k in KS:
        arrive(IZr.at[turn(zh, k)], "Iz", turn(zh, k))
    total = IZf[zh]
    for k in KS:
        total = total + IZr[turn(zh, k)].astype(F32)
    ig_o[...] = total.astype(BF)
    for copy in sent:
        copy.wait_send()


def hand_over(gg, gu, gd, ig, gg_o, gu_o, gd_o, ig_o, gg_v, gu_v, gd_v, sem):
    ways = ((gg, gg_v, gg_o), (gu, gu_v, gu_o), (gd, gd_v, gd_o))
    loads = [pltpu.make_async_copy(a, b, sem.at[0, i]) for i, (a, b, _) in enumerate(ways)]
    stores = [pltpu.make_async_copy(b, o, sem.at[1, i]) for i, (_, b, o) in enumerate(ways)]
    for load in loads:
        load.start()
    ig_o[...] = ig[...].astype(F32)[: ig_o.shape[0]].astype(BF)
    for load, store in zip(loads, stores):
        load.wait()
        store.start()
    for store in stores:
        store.wait()


def body(
    teacher_hidden,
    teacher_down,
    scale_index,
    distill_proj,
    assignment,
    student_input,
    w_gate,
    w_up,
    w_down,
):
    tokens, ft = teacher_hidden.shape
    dt, ds = distill_proj.shape
    fs = w_gate.shape[1]

    def v(shape, dtype=BF):
        return pltpu.VMEM(shape, dtype)

    dp4 = (4, 4, ROWS)
    scratch = [
        v((ft, dt)), v((dt, ds)), v((ds, fs)), v((ds, fs)), v((fs, ds)), v((16, ROWS, 16 * ROWS)), v(dp4 + (ft,)), v(dp4 + (ds,)), v((ds, 16 * ROWS)),
        v((2, 4, 32, fs), F32), v((2, 4, 32, fs), F32), v((2, 4, 32, fs), F32), v((4, 2, 32, fs)), v((4, 2, 32, fs)),
        v((4, 2, 16, 512), F32), v((4, 2, 16, 512)), v((4, 2, 16, 512)), v((4, 16, 512)), v((4, 2, 16, 512)),
        v((2, 4, 2, 16, fs)), v((2, 4, 2, 2, 16, fs)),
        v((4, 2, 16, dt), F32), v((4, 2, 16, dt), F32), v((4, 2, 16, dt), F32), v((4, 2, 16, dt)), v((4, 2, 16, dt)),
        v((4, 2, 16, dt)), v((2, 4, 2, 16, dt)),
        v((4, 4, 8, 128), F32), v((4, 2, 8, 128), F32),
        v(dp4 + (ds,), F32), v(dp4 + (ds,), F32), v(dp4 + (ds,), F32), v(dp4 + (ds,), F32),
        v(dp4 + (ds,)), v(dp4 + (ds,)),
        v((4, 2, 16, fs), F32), v((4, 2, 16, fs), F32), v((4, 2, 16, fs), F32), v((4, 2, 16, fs)), v((4, 2, 16, fs)),
        v((4, 2, 16, fs)), v((2, 4, 2, 16, fs)), v((2, 4, 2, 16, fs)), v((2, 4, 2, 16, fs)),
        v(dp4 + (ds,), F32), v(dp4 + (ds,)), v(dp4 + (ds,)), v((4, ROWS, ds), F32), v((4, ROWS, ds)), v((4, ROWS, ds)),
        pltpu.SemaphoreType.DMA((N_SEND,)), pltpu.SemaphoreType.DMA((N_RECV,)), pltpu.SemaphoreType.DMA((5,)),
    ]
    vm, hbm = pl.BlockSpec(memory_space=pltpu.VMEM), pl.BlockSpec(memory_space=pl.ANY)
    sm = pl.BlockSpec(memory_space=pltpu.SMEM)
    sds = jax.ShapeDtypeStruct
    grad_gate, grad_up, grad_down, input_grad = pl.pallas_call(
        kernel,
        out_shape=(sds((ds, fs), BF), sds((ds, fs), BF), sds((fs, ds), BF), sds((ROWS, ds), BF)),
        in_specs=[sm] * 2 + [vm] * 2 + [hbm] * 5,
        out_specs=(vm,) * 4,
        scratch_shapes=scratch,
        compiler_params=pltpu.CompilerParams(collective_id=0, has_side_effects=True, vmem_limit_bytes=56 << 20),
        name="distill_step",
    )(scale_index, assignment, teacher_hidden, student_input, teacher_down, distill_proj, w_gate, w_up, w_down)
    return pl.pallas_call(
        hand_over,
        out_shape=(sds((ds, fs), BF), sds((ds, fs), BF), sds((fs, ds), BF), sds((tokens, ds), BF)),
        in_specs=[hbm] * 3 + [vm],
        out_specs=(hbm,) * 3 + (vm,),
        scratch_shapes=[v((ds, fs)), v((ds, fs)), v((fs, ds)), pltpu.SemaphoreType.DMA((2, 3))],
        name="hand_over",
    )(grad_gate, grad_up, grad_down, input_grad)


def solution(mesh):
    placed = (
        P("dp", "mp"),
        P("mp", "dp"),
        P("mp"),
        P("dp", "mp"),
        P(),
        P("dp", "mp"),
        P("mp", "dp"),
        P("mp", "dp"),
        P("dp", "mp"),
    )
    return jax.shard_map(
        body,
        mesh=mesh,
        in_specs=placed,
        out_specs=(P("mp", "dp"), P("mp", "dp"), P("dp", "mp"), P("dp", "mp")),
        check_vma=False,
    )
```

```python
import functools

import jax
import jax.numpy as jnp
from jax import lax
from jax.experimental import pallas as pl
from jax.experimental.pallas import tpu as pltpu
from jax.sharding import PartitionSpec as P

MESH = pl.DeviceIdType.MESH
BF, F32 = jnp.bfloat16, jnp.float32
ROWS = 16
KS = (2, 1, 3)

RECV = {}
N_RECV = 0
for _name, _n in (
    ("Sz", 4), ("Tz", 4), ("Sy", 4), ("Ty", 4), ("Sc", 2), ("Tc", 2), ("Sx", 8), ("Tx", 8), ("Szl", 8), ("Tzl", 8), ("Tzg", 8),
    ("Hzl", 4), ("ABzl", 4), ("Hx", 4), ("Hc", 1), ("ABx", 4), ("ABc", 1), ("Tax", 8), ("Tac", 1),
    ("Md", 16), ("Mc", 8), ("TPy", 4), ("SPy", 4), ("Iz", 4),
):
    RECV[_name] = N_RECV
    N_RECV += _n
for _name, _earlier in (
    ("Oz", "Sz"), ("Oy", "Sy"), ("Gc", "Tc"), ("Gx", "Tx"), ("Gzl", "Tzl"), ("Gax", "Tax"), ("Gac", "Tac"), ("Iy", "Md"),
):
    RECV[_name] = RECV[_earlier]
N_SEND = 48


def dot(a, b):
    return jnp.dot(a, b, preferred_element_type=F32)


def dot_nt(a, b):
    return lax.dot_general(a, b, (((1,), (1,)), ((), ())), preferred_element_type=F32)


def dot_tn(a, b):
    return lax.dot_general(a, b, (((0,), (0,)), ((), ())), preferred_element_type=F32)


def kernel(
    index_h, assign_h, th_h, xin_h, td_h, dp_h, wg_h, wu_h, wd_h,
    gg_h, gu_h, gd_h, ig_h,
    index, assign, th, xin, gg_o, gu_o, gd_o, ig_o,
    td, dpj, wg, wu, wd, perm, TG, XG, XT,
    SCs, SCr, SOWN, SXs, SXr, SZf, SZs, SZr, HZ, ABZ, HID, AB,
    TCs, TCr, TOWN, TXs, TXr, TZs, TZr, TW, TO, AMd, AMc,
    TPf, TPs, TPr, SPf, SPs, SPr, OZ, OG,
    GCs, GCr, GOWN, GXs, GXr, GZ, HG, GG, UG, IPf, IPs, IPr, IZs, IZr,
    send_sem, recv_sem, load_sem, store_sem,
):
    d, m = lax.axis_index("dp"), lax.axis_index("mp")
    zh, y, zl, x, c = d // 4, d % 4, m // 8, (m // 2) % 4, m % 2
    oc = 1 - c

    def turn(v, k):
        return lax.rem(v + k, 4)

    def at(zh=zh, y=y, zl=zl, x=x, c=c):
        return (zh * 4 + y, zl * 8 + x * 2 + c)

    core = at(c=oc)
    x_dev = lambda v: at(x=v)
    y_dev = lambda v: at(y=v)
    zl_dev = lambda v: at(zl=v)
    zh_dev = lambda v: at(zh=v)

    sent = []

    def send(src, dst, dev, name, slot):
        if len(sent) >= N_SEND:
            sent[-N_SEND].wait_send()
        copy = pltpu.make_async_remote_copy(
            src, dst, send_sem.at[len(sent) % N_SEND], recv_sem.at[RECV[name] + slot], device_id=dev, device_id_type=MESH
        )
        copy.start()
        sent.append(copy)

    def arrive(dst, name, slot):
        pltpu.make_async_remote_copy(
            dst, dst, send_sem.at[0], recv_sem.at[RECV[name] + slot], device_id=core, device_id_type=MESH
        ).wait_recv()

    def scatter_x(own, other, out, into, n_core, n_x, r):
        arrive(other.at[:, r], n_core, r)
        for k in KS:
            v = turn(x, k)
            out[v, r] = (own[v, r] + other[v, r].astype(F32)).astype(out.dtype)
            send(out.at[v, r], into.at[x, r], x_dev(v), n_x, x * 2 + r)

    def share_zl(own, other, into, shares, n_x, n_zl, r):
        total = own[x, r] + other[x, r].astype(F32)
        for k in KS:
            arrive(into.at[turn(x, k), r], n_x, turn(x, k) * 2 + r)
        for k in KS:
            total = total + into[turn(x, k), r].astype(F32)
        shares[zl, r] = total.astype(BF)
        for k in KS:
            send(shares.at[zl, r], shares.at[zl, r], zl_dev(turn(zl, k)), n_zl, zl * 2 + r)

    def gather_x(shares, result, n_zl, n_x, n_core, r):
        for k in KS:
            arrive(shares.at[turn(zl, k), r], n_zl, turn(zl, k) * 2 + r)
        total = shares[0, r].astype(F32)
        for w in range(1, 4):
            total = total + shares[w, r].astype(F32)
        result[c, x, r] = total.astype(BF)
        mine = result.at[c, x, r]
        for k in KS:
            send(mine, mine, x_dev(turn(x, k)), n_x, x * 2 + r)
        send(mine, mine, core, n_core, 0)

    def pass_on(result, n_x, n_core, r):
        for k in KS:
            v = turn(x, k)
            arrive(result.at[c, v, r], n_x, v * 2 + r)
            send(result.at[c, v, r], result.at[c, v, r], core, n_core, 0)

    barrier = pltpu.get_barrier_semaphore()
    partners = [core]
    for k in KS:
        partners += [x_dev(turn(x, k)), at(x=turn(x, k), c=oc), zl_dev(turn(zl, k))]
    dp_group = [at(zh=turn(zh, i), y=turn(y, j)) for i in KS + (0,) for j in KS + (0,)][:-1]
    pairs = [at(x=turn(x, k), c=b) for k in KS for b in (oc, c)] + [core]
    partners += dp_group
    for p in partners:
        pl.semaphore_signal(barrier, inc=1, device_id=p, device_id_type=MESH)
    loads = [
        pltpu.make_async_copy(a, b, load_sem.at[i])
        for i, (a, b) in enumerate(
            (
                (wg_h, wg), (wu_h, wu), (td_h, td), (dp_h, dpj), (wd_h, wd),
                (xin_h, xin), (index_h, index), (th_h, th), (assign_h, assign),
            )
        )
    ]
    for load in loads[5:] + loads[:5]:
        load.start()
    stores = []

    def store(src, dst):
        stores.append(pltpu.make_async_copy(src, dst, store_sem.at[len(stores)]))
        stores[-1].start()

    tokens, ft = th.shape
    groups = index.shape[0]

    def padded(rows):
        return jnp.concatenate([rows, jnp.zeros((ROWS - tokens, rows.shape[1]), F32)], axis=0).astype(BF)

    loads[5].wait()
    XG[zh, y] = padded(xin[...].astype(F32))
    group = lax.broadcasted_iota(jnp.int32, (1, ft), 1) // (ft // groups)
    level = jnp.zeros((1, ft), jnp.int32)
    loads[6].wait()
    for i in range(groups):
        level = jnp.where(group == i, index[i], level)
    scales = jnp.full((1, ft), 0.125, F32)
    for i in range(1, 7):
        scales = jnp.where(level == i, 0.125 * 2**i, scales)
    loads[7].wait()
    TG[zh, y] = padded(th[...].astype(F32) * scales)

    def place(block, carry):
        row = lax.broadcasted_iota(jnp.int32, (ROWS, 16 * ROWS), 0)
        column = lax.broadcasted_iota(jnp.int32, (ROWS, 16 * ROWS), 1)
        source = jnp.full((ROWS, 16 * ROWS), -1, jnp.int32)
        for i in range(tokens):
            a = assign[block * tokens + i]
            source = jnp.where(row == i, lax.div(a, tokens) * ROWS + lax.rem(a, tokens), source)
        perm[block] = jnp.where(source == column, 1.0, 0.0).astype(BF)
        return carry

    loads[8].wait()
    lax.fori_loop(0, 16, place, 0)
    pl.semaphore_wait(barrier, len(partners))

    for buf, nz, ny in ((XG, "Sz", "Sy"), (TG, "Tz", "Ty")):
        own = buf.at[zh, y]
        for k in KS:
            send(own, own, zh_dev(turn(zh, k)), nz, zh)
        for k in KS:
            send(own, own, y_dev(turn(y, k)), ny, y)
    for buf, nz, ny in ((XG, "Sz", "Sy"), (TG, "Tz", "Ty")):
        for k in KS:
            z = turn(zh, k)
            arrive(buf.at[z, y], nz, z)
            for j in KS:
                send(buf.at[z, y], buf.at[z, y], y_dev(turn(y, j)), ny, y)

    for j in KS:
        arrive(XG.at[:, turn(y, j)], "Sy", turn(y, j))
    loads[0].wait()
    loads[1].wait()
    half = XG[pl.ds(2 * oc, 2)].reshape(128, -1)
    for a, w in enumerate((wg, wu)):
        SCs[a] = dot(half, w[...]).reshape(SCs.shape[1:])
        send(SCs.at[a], SCr.at[a], core, "Sc", a)
    half = XG[pl.ds(2 * c, 2)].reshape(128, -1)
    for a, w in enumerate((wg, wu)):
        SOWN[a] = dot(half, w[...]).reshape(SOWN.shape[1:])

    for j in KS:
        arrive(TG.at[:, turn(y, j)], "Ty", turn(y, j))
    loads[2].wait()
    everything = TG[...].reshape(16 * ROWS, -1)
    picked = dot(perm[pl.ds(8 * oc, 8)].reshape(128, -1), everything).astype(BF)
    TCs[...] = dot(picked, td[...]).reshape(TCs.shape)
    for r in range(2):
        send(TCs.at[:, r], TCr.at[:, r], core, "Tc", r)
    picked = dot(perm[pl.ds(8 * c, 8)].reshape(128, -1), everything).astype(BF)
    TOWN[...] = dot(picked, td[...]).reshape(TOWN.shape)

    for a in range(2):
        arrive(SCr.at[a], "Sc", a)
        for k in KS:
            v = turn(x, k)
            SXs[v, a] = (SOWN[a, v] + SCr[a, v]).astype(BF)
            send(SXs.at[v, a], SXr.at[x, a], x_dev(v), "Sx", x * 2 + a)
    for r in range(2):
        scatter_x(TOWN, TCr, TXs, TXr, "Tc", "Tx", r)
    XT[...] = XG[...].reshape(16 * ROWS, -1).T

    fs = SOWN.shape[-1]
    shift = fs - 512
    for a in range(2):
        for k in KS:
            arrive(SXr.at[turn(x, k), a], "Sx", turn(x, k) * 2 + a)
        total = SOWN[a, x] + SCr[a, x]
        for k in KS:
            total = total + SXr[turn(x, k), a].astype(F32)
        for w in range(4):
            r, h = w % 2, w // 2
            part = total[r * 16 : r * 16 + 16, h * shift : h * shift + 512]
            SZf[w, a] = part
            SZs[w, a] = part.astype(BF)
        for k in KS:
            v = turn(zl, k)
            send(SZs.at[v, a], SZr.at[zl, a], zl_dev(v), "Szl", zl * 2 + a)
    piece = TZs.shape[-1]
    for r in range(2):
        total = TOWN[x, r] + TCr[x, r]
        for k in KS:
            arrive(TXr.at[turn(x, k), r], "Tx", turn(x, k) * 2 + r)
        for k in KS:
            total = total + TXr[turn(x, k), r]
        for w in range(4):
            TZs[w, r] = total[:, w * piece : (w + 1) * piece]
        for k in KS:
            v = turn(zl, k)
            send(TZs.at[v, r], TZr.at[zl, r], zl_dev(v), "Tzl", zl * 2 + r)

    pre = []
    for a in range(2):
        for k in KS:
            arrive(SZr.at[turn(zl, k), a], "Szl", turn(zl, k) * 2 + a)
        total = SZf[zl, a]
        for k in KS:
            total = total + SZr[turn(zl, k), a].astype(F32)
        pre.append(total)
    gate, up = pre
    sig = jax.nn.sigmoid(gate)
    HZ[zl] = (gate * sig * up).astype(BF)
    for k in KS:
        send(HZ.at[zl], HZ.at[zl], zl_dev(turn(zl, k)), "Hzl", zl)
    for r in range(2):
        total = TZs[zl, r]
        for k in KS:
            arrive(TZr.at[turn(zl, k), r], "Tzl", turn(zl, k) * 2 + r)
        for k in KS:
            total = total + TZr[turn(zl, k), r]
        TW[zl, r] = total.astype(BF)
        for k in KS:
            send(TW.at[zl, r], TW.at[zl, r], zl_dev(turn(zl, k)), "Tzg", zl * 2 + r)
    ABZ[zl, 0] = (up * sig * (1.0 + gate * (1.0 - sig))).astype(BF)
    ABZ[zl, 1] = (gate * sig).astype(BF)

    for k in KS:
        arrive(HZ.at[turn(zl, k)], "Hzl", turn(zl, k))
    for r in range(2):
        HID[c, x, r, :, 0:512] = HZ[r]
        HID[c, x, r, :, 512:fs] = HZ[2 + r][:, 512 - shift :]
    for k in KS:
        send(HID.at[c, x], HID.at[c, x], x_dev(turn(x, k)), "Hx", x)
    send(HID.at[c, x], HID.at[c, x], core, "Hc", 0)
    for r in range(2):
        for k in KS:
            arrive(TW.at[turn(zl, k), r], "Tzg", turn(zl, k) * 2 + r)
        for w in range(4):
            TO[c, x, r, :, w * piece : (w + 1) * piece] = TW[w, r]
        mine = TO.at[c, x, r]
        for k in KS:
            send(mine, mine, x_dev(turn(x, k)), "Tax", x * 2 + r)
        send(mine, mine, core, "Tac", 0)
    AMd[zh, y] = jnp.full((8, 128), jnp.max(jnp.abs(TO[c, x].astype(F32))), F32)
    for p in dp_group:
        send(AMd.at[zh, y], AMd.at[zh, y], p, "Md", zh * 4 + y)

    for k in KS:
        v = turn(x, k)
        arrive(HID.at[c, v], "Hx", v)
        send(HID.at[c, v], HID.at[c, v], core, "Hc", 0)
    for r in range(2):
        pass_on(TO, "Tax", "Tac", r)

    loads[4].wait()
    arrive(HID.at[oc], "Hc", 0)
    part = dot(HID[...].reshape(16 * ROWS, -1), wd[...]).reshape(SPf.shape)
    SPf[...] = part
    SPs[...] = part.astype(BF)
    for k in KS:
        v = turn(y, k)
        send(SPs.at[:, v], SPr.at[y], y_dev(v), "SPy", y)
    loads[3].wait()
    arrive(TO.at[oc], "Tac", 0)
    part = dot(TO[...].reshape(16 * ROWS, -1), dpj[...]).reshape(TPf.shape)
    TPf[...] = part
    TPs[...] = part.astype(BF)
    for k in KS:
        v = turn(y, k)
        send(TPs.at[:, v], TPr.at[y], y_dev(v), "TPy", y)

    for i in KS + (0,):
        for j in KS + (0,):
            if i or j:
                arrive(AMd.at[turn(zh, i), turn(y, j)], "Md", turn(zh, i) * 4 + turn(y, j))
    AMc[x, c] = jnp.max(AMd[...].reshape(16, 8, 128), axis=0)
    for p in pairs:
        send(AMc.at[x, c], AMc.at[x, c], p, "Mc", x * 2 + c)
    for k in KS:
        send(ABZ.at[zl], ABZ.at[zl], zl_dev(turn(zl, k)), "ABzl", zl)

    for k in KS:
        arrive(TPr.at[turn(y, k)], "TPy", turn(y, k))
        arrive(SPr.at[turn(y, k)], "SPy", turn(y, k))
    for k in KS:
        for b in range(2):
            arrive(AMc.at[turn(x, k), b], "Mc", turn(x, k) * 2 + b)
    arrive(AMc.at[x, oc], "Mc", x * 2 + oc)
    scale = (4.0 / jnp.max(AMc[...].reshape(8, 8, 128), axis=0))[0:1, 0:1]
    halves = (oc, c)
    for j, p in enumerate(halves):
        for i in range(2):
            z = 2 * p + i
            target, student = TPf[z, y], SPf[z, y]
            for k in KS:
                target = target + TPr[turn(y, k), z].astype(F32)
                student = student + SPr[turn(y, k), z].astype(F32)
            OZ[zh, z] = ((student - target * scale) * 0.5).astype(BF)
        part_of = OZ.at[zh, pl.ds(2 * p, 2)]
        for k in KS:
            send(part_of, part_of, zh_dev(turn(zh, k)), "Oz", zh * 2 + j)
    for k in KS:
        arrive(ABZ.at[turn(zl, k)], "ABzl", turn(zl, k))
    for a in range(2):
        for r in range(2):
            AB[c, x, a, r, :, 0:512] = ABZ[r, a]
            AB[c, x, a, r, :, 512:fs] = ABZ[2 + r, a][:, 512 - shift :]
    for k in KS:
        send(AB.at[c, x], AB.at[c, x], x_dev(turn(x, k)), "ABx", x)
    send(AB.at[c, x], AB.at[c, x], core, "ABc", 0)
    for j, p in enumerate(halves):
        for k in KS:
            arrive(OZ.at[turn(zh, k), pl.ds(2 * p, 2)], "Oz", turn(zh, k) * 2 + j)
        for i in range(2):
            z = 2 * p + i
            total = OZ[0, z].astype(F32)
            for w in range(1, 4):
                total = total + OZ[w, z].astype(F32)
            OG[z, y] = total.astype(BF)
        part_of = OG.at[pl.ds(2 * p, 2), y]
        for k in KS:
            send(part_of, part_of, y_dev(turn(y, k)), "Oy", y * 2 + j)

    for k in KS:
        v = turn(x, k)
        arrive(AB.at[c, v], "ABx", v)
        send(AB.at[c, v], AB.at[c, v], core, "ABc", 0)

    for k in KS:
        arrive(OG.at[pl.ds(2 * oc, 2), turn(y, k)], "Oy", turn(y, k) * 2)
    GCs[...] = dot_nt(OG[pl.ds(2 * oc, 2)].reshape(128, -1), wd[...]).astype(BF).reshape(GCs.shape)
    for r in range(2):
        send(GCs.at[:, r], GCr.at[:, r], core, "Gc", r)
    for k in KS:
        arrive(OG.at[pl.ds(2 * c, 2), turn(y, k)], "Oy", turn(y, k) * 2 + 1)
    GOWN[...] = dot_nt(OG[pl.ds(2 * c, 2)].reshape(128, -1), wd[...]).reshape(GOWN.shape)
    for r in range(2):
        scatter_x(GOWN, GCr, GXs, GXr, "Gc", "Gx", r)
    gd_o[...] = dot_tn(HID[...].reshape(16 * ROWS, -1), OG[...].reshape(16 * ROWS, -1)).astype(BF)
    store(gd_o, gd_h)
    for r in range(2):
        share_zl(GOWN, GCr, GXr, GZ, "Gx", "Gzl", r)
    arrive(AB.at[oc], "ABc", 0)
    for r in range(2):
        gather_x(GZ, HG, "Gzl", "Gax", "Gac", r)
    for r in range(2):
        pass_on(HG, "Gax", "Gac", r)
    arrive(HG.at[oc], "Gac", 0)
    for cc in range(2):
        for v in range(4):
            g = HG[cc, v].astype(F32)
            GG[cc, v] = (g * AB[cc, v, 0].astype(F32)).astype(BF)
            UG[cc, v] = (g * AB[cc, v, 1].astype(F32)).astype(BF)

    gates, ups = GG[...].reshape(16 * ROWS, -1), UG[...].reshape(16 * ROWS, -1)
    part = (dot_nt(gates, wg[...]) + dot_nt(ups, wu[...])).reshape(IPf.shape)
    IPf[...] = part
    IPs[...] = part.astype(BF)
    for i in KS + (0,):
        z = turn(zh, i)
        for k in KS:
            v = turn(y, k)
            send(IPs.at[z, v], IPr.at[y, z], y_dev(v), "Iy", y * 4 + z)
    gg_o[...] = dot(XT[...], gates).astype(BF)
    store(gg_o, gg_h)
    for i in KS + (0,):
        z = turn(zh, i)
        for k in KS:
            arrive(IPr.at[turn(y, k), z], "Iy", turn(y, k) * 4 + z)
        total = IPf[z, y]
        for k in KS:
            total = total + IPr[turn(y, k), z].astype(F32)
        if i:
            IZs[z] = total.astype(BF)
            send(IZs.at[z], IZr.at[zh], zh_dev(z), "Iz", zh)
    gu_o[...] = dot(XT[...], ups).astype(BF)
    store(gu_o, gu_h)
    for k in KS:
        arrive(IZr.at[turn(zh, k)], "Iz", turn(zh, k))
    for k in KS:
        total = total + IZr[turn(zh, k)].astype(F32)
    ig_o[...] = total.astype(BF)
    store(ig_o, ig_h)
    for copy in sent[-N_SEND:]:
        copy.wait_send()
    for copy in stores:
        copy.wait()


def hand_over(gg, gu, gd, ig, gg_o, gu_o, gd_o, ig_o, gg_v, gu_v, gd_v, ig_v, sem):
    ways = []
    for a, b, o in ((gg, gg_v, gg_o), (gu, gu_v, gu_o), (gd, gd_v, gd_o)):
        half = a.shape[0] // 2
        ways += [(a.at[pl.ds(i * half, half)], b.at[pl.ds(i * half, half)], o.at[pl.ds(i * half, half)]) for i in range(2)]
    loads = [pltpu.make_async_copy(a, b, sem.at[0, i]) for i, (a, b, _) in enumerate(ways)]
    stores = [pltpu.make_async_copy(b, o, sem.at[1, i]) for i, (_, b, o) in enumerate(ways)]
    last = pltpu.make_async_copy(ig, ig_v, sem.at[0, len(ways)])
    for load in loads + [last]:
        load.start()
    for load, store in zip(loads, stores):
        load.wait()
        store.start()
    last.wait()
    ig_o[...] = ig_v[...].astype(F32)[: ig_o.shape[0]].astype(BF)
    for store in stores:
        store.wait()


def body(
    teacher_hidden,
    teacher_down,
    scale_index,
    distill_proj,
    assignment,
    student_input,
    w_gate,
    w_up,
    w_down,
):
    tokens, ft = teacher_hidden.shape
    dt, ds = distill_proj.shape
    fs = w_gate.shape[1]

    def v(shape, dtype=BF):
        return pltpu.VMEM(shape, dtype)

    dp4 = (4, 4, ROWS)
    scratch = [
        pltpu.SMEM(scale_index.shape, jnp.int32), pltpu.SMEM(assignment.shape, jnp.int32), v((tokens, ft)), v((tokens, ds)),
        v((ds, fs)), v((ds, fs)), v((fs, ds)), v((ROWS, ds)),
        v((ft, dt)), v((dt, ds)), v((ds, fs)), v((ds, fs)), v((fs, ds)), v((16, ROWS, 16 * ROWS)), v(dp4 + (ft,)), v(dp4 + (ds,)), v((ds, 16 * ROWS)),
        v((2, 4, 32, fs), F32), v((2, 4, 32, fs), F32), v((2, 4, 32, fs), F32), v((4, 2, 32, fs)), v((4, 2, 32, fs)),
        v((4, 2, 16, 512), F32), v((4, 2, 16, 512)), v((4, 2, 16, 512)), v((4, 16, 512)), v((4, 2, 16, 512)),
        v((2, 4, 2, 16, fs)), v((2, 4, 2, 2, 16, fs)),
        v((4, 2, 16, dt), F32), v((4, 2, 16, dt), F32), v((4, 2, 16, dt), F32), v((4, 2, 16, dt), F32), v((4, 2, 16, dt), F32),
        v((4, 2, 16, dt // 4), F32), v((4, 2, 16, dt // 4), F32), v((4, 2, 16, dt // 4)), v((2, 4, 2, 16, dt)),
        v((4, 4, 8, 128), F32), v((4, 2, 8, 128), F32),
        v(dp4 + (ds,), F32), v(dp4 + (ds,)), v(dp4 + (ds,)), v(dp4 + (ds,), F32), v(dp4 + (ds,)), v(dp4 + (ds,)),
        v(dp4 + (ds,)), v(dp4 + (ds,)),
        v((4, 2, 16, fs)), v((4, 2, 16, fs)), v((4, 2, 16, fs), F32), v((4, 2, 16, fs)), v((4, 2, 16, fs)),
        v((4, 2, 16, fs)), v((2, 4, 2, 16, fs)), v((2, 4, 2, 16, fs)), v((2, 4, 2, 16, fs)),
        v(dp4 + (ds,), F32), v(dp4 + (ds,)), v(dp4 + (ds,)), v((4, ROWS, ds)), v((4, ROWS, ds)),
        pltpu.SemaphoreType.DMA((N_SEND,)), pltpu.SemaphoreType.DMA((N_RECV,)), pltpu.SemaphoreType.DMA((9,)), pltpu.SemaphoreType.DMA((4,)),
    ]
    vm, hbm = pl.BlockSpec(memory_space=pltpu.VMEM), pl.BlockSpec(memory_space=pl.ANY)
    sds = jax.ShapeDtypeStruct
    grad_gate, grad_up, grad_down, input_grad = pl.pallas_call(
        kernel,
        out_shape=(sds((ds, fs), BF), sds((ds, fs), BF), sds((fs, ds), BF), sds((ROWS, ds), BF)),
        in_specs=[hbm] * 9,
        out_specs=(hbm,) * 4,
        scratch_shapes=scratch,
        compiler_params=pltpu.CompilerParams(collective_id=0, has_side_effects=True, vmem_limit_bytes=56 << 20),
        name="distill_step",
    )(scale_index, assignment, teacher_hidden, student_input, teacher_down, distill_proj, w_gate, w_up, w_down)
    return pl.pallas_call(
        hand_over,
        out_shape=(sds((ds, fs), BF), sds((ds, fs), BF), sds((fs, ds), BF), sds((tokens, ds), BF)),
        in_specs=[hbm] * 4,
        out_specs=(hbm,) * 3 + (vm,),
        scratch_shapes=[v((ds, fs)), v((ds, fs)), v((fs, ds)), v((ROWS, ds)), pltpu.SemaphoreType.DMA((2, 7))],
        name="hand_over",
    )(grad_gate, grad_up, grad_down, input_grad)


def solution(mesh):
    placed = (
        P("dp", "mp"),
        P("mp", "dp"),
        P("mp"),
        P("dp", "mp"),
        P(),
        P("dp", "mp"),
        P("mp", "dp"),
        P("mp", "dp"),
        P("dp", "mp"),
    )
    return jax.shard_map(
        body,
        mesh=mesh,
        in_specs=placed,
        out_specs=(P("mp", "dp"), P("mp", "dp"), P("dp", "mp"), P("dp", "mp")),
        check_vma=False,
    )
```

```python
import functools

import jax
import jax.numpy as jnp
from jax import lax
from jax.experimental import pallas as pl
from jax.experimental.pallas import tpu as pltpu
from jax.sharding import PartitionSpec as P

MESH = pl.DeviceIdType.MESH
BF, F32 = jnp.bfloat16, jnp.float32
ROWS = 16
KS = (2, 1, 3)

RECV = {}
N_RECV = 0
for _name, _n in (
    ("Sz", 4), ("Tz", 8), ("Sy", 4), ("Ty", 4), ("Sc", 2), ("Tc", 2), ("Sx", 8), ("Tx", 8), ("Szl", 8), ("Tzl", 8), ("Tzg", 8),
    ("Hzl", 4), ("ABzl", 4), ("Hx", 4), ("Hc", 1), ("ABx", 4), ("ABc", 1), ("Tax", 8), ("Tac", 1),
    ("Md", 16), ("Mc", 8), ("TPy", 4), ("SPy", 4), ("Iz", 4),
):
    RECV[_name] = N_RECV
    N_RECV += _n
for _name, _earlier in (
    ("Oz", "Sz"), ("Oy", "Sy"), ("Gc", "Tc"), ("Gx", "Tx"), ("Gzl", "Tzl"), ("Gax", "Tax"), ("Gac", "Tac"), ("Iy", "Md"),
):
    RECV[_name] = RECV[_earlier]
N_SEND = 48


def dot(a, b):
    return jnp.dot(a, b, preferred_element_type=F32)


def dot_nt(a, b):
    return lax.dot_general(a, b, (((1,), (1,)), ((), ())), preferred_element_type=F32)


def dot_tn(a, b):
    return lax.dot_general(a, b, (((0,), (0,)), ((), ())), preferred_element_type=F32)


def kernel(
    index_h, assign_h, th_h, xin_h, td_h, dp_h, wg_h, wu_h, wd_h,
    gg_h, gu_h, gd_h, ig_h,
    index, assign, th, xin, gg_o, gu_o, gd_o, ig_o,
    td, dpj, wg, wu, wd, perm, TG, XG, XT,
    SCs, SCr, SOWN, SXs, SXr, SZf, SZs, SZr, HZ, ABZ, HID, AB,
    TCs, TCr, TOWN, TXs, TXr, TZs, TZr, TW, TO, AMd, AMc,
    TPf, TPs, TPr, SPf, SPs, SPr, OZ, OG,
    GCs, GCr, GOWN, GXs, GXr, GZ, HG, GG, UG, IPf, IPs, IPr, IZs, IZr,
    send_sem, recv_sem, load_sem, store_sem,
):
    d, m = lax.axis_index("dp"), lax.axis_index("mp")
    zh, y, zl, x, c = d // 4, d % 4, m // 8, (m // 2) % 4, m % 2
    oc = 1 - c

    def turn(v, k):
        return lax.rem(v + k, 4)

    def at(zh=zh, y=y, zl=zl, x=x, c=c):
        return (zh * 4 + y, zl * 8 + x * 2 + c)

    core = at(c=oc)
    x_dev = lambda v: at(x=v)
    y_dev = lambda v: at(y=v)
    zl_dev = lambda v: at(zl=v)
    zh_dev = lambda v: at(zh=v)

    sent = []

    def send(src, dst, dev, name, slot):
        if len(sent) >= N_SEND:
            sent[-N_SEND].wait_send()
        copy = pltpu.make_async_remote_copy(
            src, dst, send_sem.at[len(sent) % N_SEND], recv_sem.at[RECV[name] + slot], device_id=dev, device_id_type=MESH
        )
        copy.start()
        sent.append(copy)

    def arrive(dst, name, slot):
        pltpu.make_async_remote_copy(
            dst, dst, send_sem.at[0], recv_sem.at[RECV[name] + slot], device_id=core, device_id_type=MESH
        ).wait_recv()

    def scatter_x(own, other, out, into, n_core, n_x, r):
        arrive(other.at[:, r], n_core, r)
        for k in KS:
            v = turn(x, k)
            out[v, r] = (own[v, r] + other[v, r].astype(F32)).astype(out.dtype)
            send(out.at[v, r], into.at[x, r], x_dev(v), n_x, x * 2 + r)

    def share_zl(own, other, into, shares, n_x, n_zl, r):
        total = own[x, r] + other[x, r].astype(F32)
        for k in KS:
            arrive(into.at[turn(x, k), r], n_x, turn(x, k) * 2 + r)
        for k in KS:
            total = total + into[turn(x, k), r].astype(F32)
        shares[zl, r] = total.astype(BF)
        for k in KS:
            send(shares.at[zl, r], shares.at[zl, r], zl_dev(turn(zl, k)), n_zl, zl * 2 + r)

    def gather_x(shares, result, n_zl, n_x, n_core, r):
        for k in KS:
            arrive(shares.at[turn(zl, k), r], n_zl, turn(zl, k) * 2 + r)
        total = shares[0, r].astype(F32)
        for w in range(1, 4):
            total = total + shares[w, r].astype(F32)
        result[c, x, r] = total.astype(BF)
        mine = result.at[c, x, r]
        for k in KS:
            send(mine, mine, x_dev(turn(x, k)), n_x, x * 2 + r)
        send(mine, mine, core, n_core, 0)

    def pass_on(result, n_x, n_core, r):
        for k in KS:
            v = turn(x, k)
            arrive(result.at[c, v, r], n_x, v * 2 + r)
            send(result.at[c, v, r], result.at[c, v, r], core, n_core, 0)

    barrier = pltpu.get_barrier_semaphore()
    partners = [core]
    for k in KS:
        partners += [x_dev(turn(x, k)), at(x=turn(x, k), c=oc), zl_dev(turn(zl, k))]
    dp_group = [at(zh=turn(zh, i), y=turn(y, j)) for i in KS + (0,) for j in KS + (0,)][:-1]
    pairs = [at(x=turn(x, k), c=b) for k in KS for b in (oc, c)] + [core]
    partners = dp_group + partners
    for p in partners:
        pl.semaphore_signal(barrier, inc=1, device_id=p, device_id_type=MESH)
    loads = [
        pltpu.make_async_copy(a, b, load_sem.at[i])
        for i, (a, b) in enumerate(
            (
                (wg_h, wg), (wu_h, wu), (td_h, td), (dp_h, dpj), (wd_h, wd),
                (xin_h, xin), (index_h, index), (th_h, th), (assign_h, assign),
            )
        )
    ]
    for load in loads[5:] + loads[:5]:
        load.start()
    stores = []

    def store(src, dst):
        stores.append(pltpu.make_async_copy(src, dst, store_sem.at[len(stores)]))
        stores[-1].start()

    tokens, ft = th.shape
    groups = index.shape[0]

    def padded(rows):
        return jnp.concatenate([rows, jnp.zeros((ROWS - tokens, rows.shape[1]), F32)], axis=0).astype(BF)

    loads[5].wait()
    XG[zh, y] = padded(xin[...].astype(F32))
    group = lax.broadcasted_iota(jnp.int32, (1, ft), 1) // (ft // groups)
    level = jnp.zeros((1, ft), jnp.int32)
    loads[6].wait()
    for i in range(groups):
        level = jnp.where(group == i, index[i], level)
    scales = jnp.full((1, ft), 0.125, F32)
    for i in range(1, 7):
        scales = jnp.where(level == i, 0.125 * 2**i, scales)
    loads[7].wait()
    TG[zh, y] = padded(th[...].astype(F32) * scales)

    def place(block, carry):
        row = lax.broadcasted_iota(jnp.int32, (ROWS, 16 * ROWS), 0)
        column = lax.broadcasted_iota(jnp.int32, (ROWS, 16 * ROWS), 1)
        source = jnp.full((ROWS, 16 * ROWS), -1, jnp.int32)
        for i in range(tokens):
            a = assign[block * tokens + i]
            source = jnp.where(row == i, lax.div(a, tokens) * ROWS + lax.rem(a, tokens), source)
        perm[block] = jnp.where(source == column, 1.0, 0.0).astype(BF)
        return carry

    loads[8].wait()
    lax.fori_loop(0, 16, place, 0)
    pl.semaphore_wait(barrier, len(partners))

    def columns(buf, z, low, high):
        return buf.at[z, y, :, pl.ds(low, high - low)]

    parts = ((XG, "Sz", "Sy", 0, xin.shape[1], 0), (TG, "Tz", "Ty", 0, ft, 0))
    for buf, nz, ny, low, high, slot in parts:
        own = columns(buf, zh, low, high)
        for k in KS:
            send(own, own, zh_dev(turn(zh, k)), nz, zh + slot)
    for buf, ny in ((XG, "Sy"), (TG, "Ty")):
        for k in KS:
            send(buf.at[zh, y], buf.at[zh, y], y_dev(turn(y, k)), ny, y)
    for buf, nz, ny, low, high, slot in parts:
        for k in KS:
            z = turn(zh, k)
            block = columns(buf, z, low, high)
            arrive(block, nz, z + slot)
            for j in KS:
                send(block, block, y_dev(turn(y, j)), ny, y)

    for j in KS:
        arrive(XG.at[:, turn(y, j)], "Sy", turn(y, j))
    loads[0].wait()
    loads[1].wait()
    half = XG[pl.ds(2 * oc, 2)].reshape(128, -1)
    for a, w in enumerate((wg, wu)):
        SCs[a] = dot(half, w[...]).reshape(SCs.shape[1:])
        send(SCs.at[a], SCr.at[a], core, "Sc", a)
    half = XG[pl.ds(2 * c, 2)].reshape(128, -1)
    for a, w in enumerate((wg, wu)):
        SOWN[a] = dot(half, w[...]).reshape(SOWN.shape[1:])

    for j in KS:
        arrive(TG.at[:, turn(y, j)], "Ty", turn(y, j))
    loads[2].wait()
    everything = TG[...].reshape(16 * ROWS, -1)
    picked = dot(perm[pl.ds(8 * oc, 8)].reshape(128, -1), everything).astype(BF)
    TCs[...] = dot(picked, td[...]).reshape(TCs.shape)
    for r in range(2):
        send(TCs.at[:, r], TCr.at[:, r], core, "Tc", r)
    picked = dot(perm[pl.ds(8 * c, 8)].reshape(128, -1), everything).astype(BF)
    TOWN[...] = dot(picked, td[...]).reshape(TOWN.shape)

    for a in range(2):
        arrive(SCr.at[a], "Sc", a)
        for k in KS:
            v = turn(x, k)
            SXs[v, a] = (SOWN[a, v] + SCr[a, v]).astype(BF)
            send(SXs.at[v, a], SXr.at[x, a], x_dev(v), "Sx", x * 2 + a)
    for r in range(2):
        scatter_x(TOWN, TCr, TXs, TXr, "Tc", "Tx", r)
    XT[...] = XG[...].reshape(16 * ROWS, -1).T

    fs = SOWN.shape[-1]
    shift = fs - 512
    for a in range(2):
        for k in KS:
            arrive(SXr.at[turn(x, k), a], "Sx", turn(x, k) * 2 + a)
        total = SOWN[a, x] + SCr[a, x]
        for k in KS:
            total = total + SXr[turn(x, k), a].astype(F32)
        for w in range(4):
            r, h = w % 2, w // 2
            part = total[r * 16 : r * 16 + 16, h * shift : h * shift + 512]
            SZf[w, a] = part
            SZs[w, a] = part.astype(BF)
        for k in KS:
            v = turn(zl, k)
            send(SZs.at[v, a], SZr.at[zl, a], zl_dev(v), "Szl", zl * 2 + a)
    piece = TZs.shape[-1]
    for r in range(2):
        total = TOWN[x, r] + TCr[x, r]
        for k in KS:
            arrive(TXr.at[turn(x, k), r], "Tx", turn(x, k) * 2 + r)
        for k in KS:
            total = total + TXr[turn(x, k), r]
        for w in range(4):
            TZs[w, r] = total[:, w * piece : (w + 1) * piece]
        for k in KS:
            v = turn(zl, k)
            send(TZs.at[v, r], TZr.at[zl, r], zl_dev(v), "Tzl", zl * 2 + r)

    pre = []
    for a in range(2):
        for k in KS:
            arrive(SZr.at[turn(zl, k), a], "Szl", turn(zl, k) * 2 + a)
        total = SZf[zl, a]
        for k in KS:
            total = total + SZr[turn(zl, k), a].astype(F32)
        pre.append(total)
    gate, up = pre
    sig = jax.nn.sigmoid(gate)
    HZ[zl] = (gate * sig * up).astype(BF)
    for k in KS:
        send(HZ.at[zl], HZ.at[zl], zl_dev(turn(zl, k)), "Hzl", zl)
    for r in range(2):
        total = TZs[zl, r]
        for k in KS:
            arrive(TZr.at[turn(zl, k), r], "Tzl", turn(zl, k) * 2 + r)
        for k in KS:
            total = total + TZr[turn(zl, k), r]
        TW[zl, r] = total.astype(BF)
        for k in KS:
            send(TW.at[zl, r], TW.at[zl, r], zl_dev(turn(zl, k)), "Tzg", zl * 2 + r)
    ABZ[zl, 0] = (up * sig * (1.0 + gate * (1.0 - sig))).astype(BF)
    ABZ[zl, 1] = (gate * sig).astype(BF)

    for k in KS:
        arrive(HZ.at[turn(zl, k)], "Hzl", turn(zl, k))
    for r in range(2):
        HID[c, x, r, :, 0:512] = HZ[r]
        HID[c, x, r, :, 512:fs] = HZ[2 + r][:, 512 - shift :]
    for k in KS:
        send(HID.at[c, x], HID.at[c, x], x_dev(turn(x, k)), "Hx", x)
    send(HID.at[c, x], HID.at[c, x], core, "Hc", 0)
    for r in range(2):
        for k in KS:
            arrive(TW.at[turn(zl, k), r], "Tzg", turn(zl, k) * 2 + r)
        for w in range(4):
            TO[c, x, r, :, w * piece : (w + 1) * piece] = TW[w, r]
        mine = TO.at[c, x, r]
        for k in KS:
            send(mine, mine, x_dev(turn(x, k)), "Tax", x * 2 + r)
        send(mine, mine, core, "Tac", 0)
    AMd[zh, y] = jnp.full((8, 128), jnp.max(jnp.abs(TW[...].astype(F32))), F32)
    for p in dp_group:
        send(AMd.at[zh, y], AMd.at[zh, y], p, "Md", zh * 4 + y)

    for k in KS:
        v = turn(x, k)
        arrive(HID.at[c, v], "Hx", v)
        send(HID.at[c, v], HID.at[c, v], core, "Hc", 0)
    def product(rows, weights, full, rounded, half):
        out = dot(rows[half].reshape(8 * ROWS, -1), weights[...]).reshape(2, 4, ROWS, -1)
        full[pl.ds(2 * half, 2)] = out
        rounded[pl.ds(2 * half, 2)] = out.astype(BF)

    def spread(rounded, into, name):
        for k in KS:
            v = turn(y, k)
            send(rounded.at[:, v], into.at[y], y_dev(v), name, y)

    loads[4].wait()
    product(HID, wd, SPf, SPs, c)
    for r in range(2):
        pass_on(TO, "Tax", "Tac", r)
    arrive(HID.at[oc], "Hc", 0)
    product(HID, wd, SPf, SPs, oc)
    spread(SPs, SPr, "SPy")
    loads[3].wait()
    product(TO, dpj, TPf, TPs, c)
    arrive(TO.at[oc], "Tac", 0)
    product(TO, dpj, TPf, TPs, oc)
    spread(TPs, TPr, "TPy")

    for i in KS + (0,):
        for j in KS + (0,):
            if i or j:
                arrive(AMd.at[turn(zh, i), turn(y, j)], "Md", turn(zh, i) * 4 + turn(y, j))
    AMc[x, c] = jnp.max(AMd[...].reshape(16, 8, 128), axis=0)
    for p in pairs:
        send(AMc.at[x, c], AMc.at[x, c], p, "Mc", x * 2 + c)
    for k in KS:
        send(ABZ.at[zl], ABZ.at[zl], zl_dev(turn(zl, k)), "ABzl", zl)

    for k in KS:
        arrive(TPr.at[turn(y, k)], "TPy", turn(y, k))
        arrive(SPr.at[turn(y, k)], "SPy", turn(y, k))
    for k in KS:
        for b in range(2):
            arrive(AMc.at[turn(x, k), b], "Mc", turn(x, k) * 2 + b)
    arrive(AMc.at[x, oc], "Mc", x * 2 + oc)
    scale = (4.0 / jnp.max(AMc[...].reshape(8, 8, 128), axis=0))[0:1, 0:1]
    halves = (oc, c)
    for j, p in enumerate(halves):
        for i in range(2):
            z = 2 * p + i
            target, student = TPf[z, y], SPf[z, y]
            for k in KS:
                target = target + TPr[turn(y, k), z].astype(F32)
                student = student + SPr[turn(y, k), z].astype(F32)
            OZ[zh, z] = ((student - target * scale) * 0.5).astype(BF)
        part_of = OZ.at[zh, pl.ds(2 * p, 2)]
        for k in KS:
            send(part_of, part_of, zh_dev(turn(zh, k)), "Oz", zh * 2 + j)
    for k in KS:
        arrive(ABZ.at[turn(zl, k)], "ABzl", turn(zl, k))
    for a in range(2):
        for r in range(2):
            AB[c, x, a, r, :, 0:512] = ABZ[r, a]
            AB[c, x, a, r, :, 512:fs] = ABZ[2 + r, a][:, 512 - shift :]
    for k in KS:
        send(AB.at[c, x], AB.at[c, x], x_dev(turn(x, k)), "ABx", x)
    send(AB.at[c, x], AB.at[c, x], core, "ABc", 0)
    for j, p in enumerate(halves):
        for k in KS:
            arrive(OZ.at[turn(zh, k), pl.ds(2 * p, 2)], "Oz", turn(zh, k) * 2 + j)
        for i in range(2):
            z = 2 * p + i
            total = OZ[0, z].astype(F32)
            for w in range(1, 4):
                total = total + OZ[w, z].astype(F32)
            OG[z, y] = total.astype(BF)
        part_of = OG.at[pl.ds(2 * p, 2), y]
        for k in KS:
            send(part_of, part_of, y_dev(turn(y, k)), "Oy", y * 2 + j)

    for k in KS:
        v = turn(x, k)
        arrive(AB.at[c, v], "ABx", v)
        send(AB.at[c, v], AB.at[c, v], core, "ABc", 0)

    for k in KS:
        arrive(OG.at[pl.ds(2 * oc, 2), turn(y, k)], "Oy", turn(y, k) * 2)
    GCs[...] = dot_nt(OG[pl.ds(2 * oc, 2)].reshape(128, -1), wd[...]).astype(BF).reshape(GCs.shape)
    for r in range(2):
        send(GCs.at[:, r], GCr.at[:, r], core, "Gc", r)
    for k in KS:
        arrive(OG.at[pl.ds(2 * c, 2), turn(y, k)], "Oy", turn(y, k) * 2 + 1)
    GOWN[...] = dot_nt(OG[pl.ds(2 * c, 2)].reshape(128, -1), wd[...]).reshape(GOWN.shape)
    for r in range(2):
        scatter_x(GOWN, GCr, GXs, GXr, "Gc", "Gx", r)
    gd_o[...] = dot_tn(HID[...].reshape(16 * ROWS, -1), OG[...].reshape(16 * ROWS, -1)).astype(BF)
    store(gd_o, gd_h)
    for r in range(2):
        share_zl(GOWN, GCr, GXr, GZ, "Gx", "Gzl", r)
    for r in range(2):
        gather_x(GZ, HG, "Gzl", "Gax", "Gac", r)
    for r in range(2):
        pass_on(HG, "Gax", "Gac", r)

    def input_part(half):
        for v in range(4):
            g = HG[half, v].astype(F32)
            GG[half, v] = (g * AB[half, v, 0].astype(F32)).astype(BF)
            UG[half, v] = (g * AB[half, v, 1].astype(F32)).astype(BF)
        part = dot_nt(GG[half].reshape(8 * ROWS, -1), wg[...]) + dot_nt(UG[half].reshape(8 * ROWS, -1), wu[...])
        part = part.reshape(2, 4, ROWS, -1)
        IPf[pl.ds(2 * half, 2)] = part
        IPs[pl.ds(2 * half, 2)] = part.astype(BF)
        for i in range(2):
            z = 2 * half + i
            for k in KS:
                v = turn(y, k)
                send(IPs.at[z, v], IPr.at[y, z], y_dev(v), "Iy", y * 4 + z)

    input_part(c)
    arrive(AB.at[oc], "ABc", 0)
    arrive(HG.at[oc], "Gac", 0)
    input_part(oc)
    gates, ups = GG[...].reshape(16 * ROWS, -1), UG[...].reshape(16 * ROWS, -1)
    gg_o[...] = dot(XT[...], gates).astype(BF)
    store(gg_o, gg_h)
    for i in KS + (0,):
        z = turn(zh, i)
        for k in KS:
            arrive(IPr.at[turn(y, k), z], "Iy", turn(y, k) * 4 + z)
        total = IPf[z, y]
        for k in KS:
            total = total + IPr[turn(y, k), z].astype(F32)
        if i:
            IZs[z] = total.astype(BF)
            send(IZs.at[z], IZr.at[zh], zh_dev(z), "Iz", zh)
    gu_o[...] = dot(XT[...], ups).astype(BF)
    store(gu_o, gu_h)
    for k in KS:
        arrive(IZr.at[turn(zh, k)], "Iz", turn(zh, k))
    for k in KS:
        total = total + IZr[turn(zh, k)].astype(F32)
    ig_o[...] = total.astype(BF)
    store(ig_o, ig_h)
    for copy in sent[-N_SEND:]:
        copy.wait_send()
    for copy in stores:
        copy.wait()


def hand_over(gg, gu, gd, ig, gg_o, gu_o, gd_o, ig_o, gg_v, gu_v, gd_v, ig_v, sem):
    ways = []
    for a, b, o in ((gg, gg_v, gg_o), (gu, gu_v, gu_o), (gd, gd_v, gd_o)):
        part = a.shape[0] // 2
        ways += [tuple(r.at[pl.ds(i * part, part)] for r in (a, b, o)) for i in range(2)]
    loads = [pltpu.make_async_copy(a, b, sem.at[0, i]) for i, (a, b, _) in enumerate(ways)]
    stores = [pltpu.make_async_copy(b, o, sem.at[1, i]) for i, (_, b, o) in enumerate(ways)]
    last = pltpu.make_async_copy(ig, ig_v, sem.at[0, len(ways)])
    for load in loads + [last]:
        load.start()
    for load, store in zip(loads, stores):
        load.wait()
        store.start()
    last.wait()
    ig_o[...] = ig_v[...].astype(F32)[: ig_o.shape[0]].astype(BF)
    for store in stores:
        store.wait()


def body(
    teacher_hidden,
    teacher_down,
    scale_index,
    distill_proj,
    assignment,
    student_input,
    w_gate,
    w_up,
    w_down,
):
    tokens, ft = teacher_hidden.shape
    dt, ds = distill_proj.shape
    fs = w_gate.shape[1]

    def v(shape, dtype=BF):
        return pltpu.VMEM(shape, dtype)

    dp4 = (4, 4, ROWS)
    scratch = [
        pltpu.SMEM(scale_index.shape, jnp.int32), pltpu.SMEM(assignment.shape, jnp.int32), v((tokens, ft)), v((tokens, ds)),
        v((ds, fs)), v((ds, fs)), v((fs, ds)), v((ROWS, ds)),
        v((ft, dt)), v((dt, ds)), v((ds, fs)), v((ds, fs)), v((fs, ds)), v((16, ROWS, 16 * ROWS)), v(dp4 + (ft,)), v(dp4 + (ds,)), v((ds, 16 * ROWS)),
        v((2, 4, 32, fs), F32), v((2, 4, 32, fs), F32), v((2, 4, 32, fs), F32), v((4, 2, 32, fs)), v((4, 2, 32, fs)),
        v((4, 2, 16, 512), F32), v((4, 2, 16, 512)), v((4, 2, 16, 512)), v((4, 16, 512)), v((4, 2, 16, 512)),
        v((2, 4, 2, 16, fs)), v((2, 4, 2, 2, 16, fs)),
        v((4, 2, 16, dt), F32), v((4, 2, 16, dt), F32), v((4, 2, 16, dt), F32), v((4, 2, 16, dt), F32), v((4, 2, 16, dt), F32),
        v((4, 2, 16, dt // 4), F32), v((4, 2, 16, dt // 4), F32), v((4, 2, 16, dt // 4)), v((2, 4, 2, 16, dt)),
        v((4, 4, 8, 128), F32), v((4, 2, 8, 128), F32),
        v(dp4 + (ds,), F32), v(dp4 + (ds,)), v(dp4 + (ds,)), v(dp4 + (ds,), F32), v(dp4 + (ds,)), v(dp4 + (ds,)),
        v(dp4 + (ds,)), v(dp4 + (ds,)),
        v((4, 2, 16, fs)), v((4, 2, 16, fs)), v((4, 2, 16, fs), F32), v((4, 2, 16, fs)), v((4, 2, 16, fs)),
        v((4, 2, 16, fs)), v((2, 4, 2, 16, fs)), v((2, 4, 2, 16, fs)), v((2, 4, 2, 16, fs)),
        v(dp4 + (ds,), F32), v(dp4 + (ds,)), v(dp4 + (ds,)), v((4, ROWS, ds)), v((4, ROWS, ds)),
        pltpu.SemaphoreType.DMA((N_SEND,)), pltpu.SemaphoreType.DMA((N_RECV,)), pltpu.SemaphoreType.DMA((9,)), pltpu.SemaphoreType.DMA((4,)),
    ]
    vm, hbm = pl.BlockSpec(memory_space=pltpu.VMEM), pl.BlockSpec(memory_space=pl.ANY)
    sds = jax.ShapeDtypeStruct
    grad_gate, grad_up, grad_down, input_grad = pl.pallas_call(
        kernel,
        out_shape=(sds((ds, fs), BF), sds((ds, fs), BF), sds((fs, ds), BF), sds((ROWS, ds), BF)),
        in_specs=[hbm] * 9,
        out_specs=(hbm,) * 4,
        scratch_shapes=scratch,
        compiler_params=pltpu.CompilerParams(collective_id=0, has_side_effects=True, vmem_limit_bytes=56 << 20),
        name="distill_step",
    )(scale_index, assignment, teacher_hidden, student_input, teacher_down, distill_proj, w_gate, w_up, w_down)
    return pl.pallas_call(
        hand_over,
        out_shape=(sds((ds, fs), BF), sds((ds, fs), BF), sds((fs, ds), BF), sds((tokens, ds), BF)),
        in_specs=[hbm] * 4,
        out_specs=(hbm,) * 3 + (vm,),
        scratch_shapes=[v((ds, fs)), v((ds, fs)), v((fs, ds)), v((ROWS, ds)), pltpu.SemaphoreType.DMA((2, 7))],
        name="hand_over",
    )(grad_gate, grad_up, grad_down, input_grad)


def solution(mesh):
    placed = (
        P("dp", "mp"),
        P("mp", "dp"),
        P("mp"),
        P("dp", "mp"),
        P(),
        P("dp", "mp"),
        P("mp", "dp"),
        P("mp", "dp"),
        P("dp", "mp"),
    )
    return jax.shard_map(
        body,
        mesh=mesh,
        in_specs=placed,
        out_specs=(P("mp", "dp"), P("mp", "dp"), P("dp", "mp"), P("dp", "mp")),
        check_vma=False,
    )
```

```python
import functools

import jax
import jax.numpy as jnp
from jax import lax
from jax.experimental import pallas as pl
from jax.experimental.pallas import tpu as pltpu
from jax.sharding import PartitionSpec as P

MESH = pl.DeviceIdType.MESH
BF, F32 = jnp.bfloat16, jnp.float32
ROWS = 16
KS = (2, 1, 3)

RECV = {}
N_RECV = 0
for _name, _n in (
    ("Sz", 4), ("Tz", 8), ("Sy", 4), ("Ty", 4), ("Sc", 2), ("Tc", 2), ("Sx", 8), ("Tx", 8), ("Szl", 8), ("Tzl", 8), ("Tzg", 8),
    ("Hzl", 4), ("ABzl", 4), ("Hx", 4), ("Hc", 1), ("ABx", 4), ("ABc", 1), ("Tax", 8), ("Tac", 1),
    ("Md", 16), ("Mc", 8), ("TPy", 4), ("SPy", 4), ("Iz", 4),
):
    RECV[_name] = N_RECV
    N_RECV += _n
for _name, _earlier in (
    ("Oz", "Sz"), ("Oy", "Sy"), ("Gc", "Tc"), ("Gx", "Tx"), ("Gzl", "Tzl"), ("Gax", "Tax"), ("Gac", "Tac"), ("Iy", "Md"),
):
    RECV[_name] = RECV[_earlier]
N_SEND = 48


def dot(a, b):
    return jnp.dot(a, b, preferred_element_type=F32)


def dot_nt(a, b):
    return lax.dot_general(a, b, (((1,), (1,)), ((), ())), preferred_element_type=F32)


def dot_tn(a, b):
    return lax.dot_general(a, b, (((0,), (0,)), ((), ())), preferred_element_type=F32)


def kernel(
    index_h, assign_h, th_h, xin_h, td_h, dp_h, wg_h, wu_h, wd_h,
    gg_h, gu_h, gd_h, ig_h,
    index, assign, th, xin, gg_o, gu_o, gd_o, ig_o,
    td, dpj, wg, wu, wd, perm, TG, XG, XT,
    SCs, SCr, SOWN, SXs, SXr, SZf, SZs, SZr, HZ, ABZ, HID, AB,
    TCs, TCr, TOWN, TXs, TXr, TZs, TZr, TW, TO, AMd, AMc,
    TPf, TPs, TPr, SPf, SPs, SPr, OZ, OG,
    GCs, GCr, GOWN, GXs, GXr, GZ, HG, GG, UG, IPf, IPs, IPr, IZs, IZr,
    send_sem, recv_sem, load_sem, store_sem,
):
    d, m = lax.axis_index("dp"), lax.axis_index("mp")
    zh, y, zl, x, c = d // 4, d % 4, m // 8, (m // 2) % 4, m % 2
    oc = 1 - c

    def turn(v, k):
        return lax.rem(v + k, 4)

    def at(zh=zh, y=y, zl=zl, x=x, c=c):
        return (zh * 4 + y, zl * 8 + x * 2 + c)

    core = at(c=oc)
    x_dev = lambda v: at(x=v)
    y_dev = lambda v: at(y=v)
    zl_dev = lambda v: at(zl=v)
    zh_dev = lambda v: at(zh=v)

    sent = []

    def send(src, dst, dev, name, slot):
        if len(sent) >= N_SEND:
            sent[-N_SEND].wait_send()
        copy = pltpu.make_async_remote_copy(
            src, dst, send_sem.at[len(sent) % N_SEND], recv_sem.at[RECV[name] + slot], device_id=dev, device_id_type=MESH
        )
        copy.start()
        sent.append(copy)

    def arrive(dst, name, slot):
        pltpu.make_async_remote_copy(
            dst, dst, send_sem.at[0], recv_sem.at[RECV[name] + slot], device_id=core, device_id_type=MESH
        ).wait_recv()

    def scatter_x(own, other, out, into, n_core, n_x, r):
        arrive(other.at[:, r], n_core, r)
        for k in KS:
            v = turn(x, k)
            out[v, r] = (own[v, r] + other[v, r].astype(F32)).astype(out.dtype)
            send(out.at[v, r], into.at[x, r], x_dev(v), n_x, x * 2 + r)

    def share_zl(own, other, into, shares, n_x, n_zl, r):
        total = own[x, r] + other[x, r].astype(F32)
        for k in KS:
            arrive(into.at[turn(x, k), r], n_x, turn(x, k) * 2 + r)
        for k in KS:
            total = total + into[turn(x, k), r].astype(F32)
        shares[zl, r] = total.astype(BF)
        for k in KS:
            send(shares.at[zl, r], shares.at[zl, r], zl_dev(turn(zl, k)), n_zl, zl * 2 + r)

    def gather_x(shares, result, n_zl, n_x, n_core, r):
        for k in KS:
            arrive(shares.at[turn(zl, k), r], n_zl, turn(zl, k) * 2 + r)
        total = shares[0, r].astype(F32)
        for w in range(1, 4):
            total = total + shares[w, r].astype(F32)
        result[c, x, r] = total.astype(BF)
        mine = result.at[c, x, r]
        for k in KS:
            send(mine, mine, x_dev(turn(x, k)), n_x, x * 2 + r)
        send(mine, mine, core, n_core, 0)

    def pass_on(result, n_x, n_core, r):
        for k in KS:
            v = turn(x, k)
            arrive(result.at[c, v, r], n_x, v * 2 + r)
            send(result.at[c, v, r], result.at[c, v, r], core, n_core, 0)

    barrier = pltpu.get_barrier_semaphore()
    partners = [core]
    for k in KS:
        partners += [x_dev(turn(x, k)), at(x=turn(x, k), c=oc), zl_dev(turn(zl, k))]
    dp_group = [at(zh=turn(zh, i), y=turn(y, j)) for i in KS + (0,) for j in KS + (0,)][:-1]
    pairs = [at(x=turn(x, k), c=b) for k in KS for b in (oc, c)] + [core]
    partners = dp_group + partners
    for p in partners:
        pl.semaphore_signal(barrier, inc=1, device_id=p, device_id_type=MESH)
    loads = [
        pltpu.make_async_copy(a, b, load_sem.at[i])
        for i, (a, b) in enumerate(
            (
                (wg_h, wg), (wu_h, wu), (td_h, td), (dp_h, dpj), (wd_h, wd),
                (xin_h, xin), (index_h, index), (th_h, th), (assign_h, assign),
            )
        )
    ]
    for load in loads[5:] + loads[:5]:
        load.start()
    stores = []

    def store(src, dst):
        stores.append(pltpu.make_async_copy(src, dst, store_sem.at[len(stores)]))
        stores[-1].start()

    tokens, ft = th.shape
    groups = index.shape[0]

    def padded(rows):
        return jnp.concatenate([rows, jnp.zeros((ROWS - tokens, rows.shape[1]), F32)], axis=0).astype(BF)

    loads[5].wait()
    XG[zh, y] = padded(xin[...].astype(F32))
    group = lax.broadcasted_iota(jnp.int32, (1, ft), 1) // (ft // groups)
    level = jnp.zeros((1, ft), jnp.int32)
    loads[6].wait()
    for i in range(groups):
        level = jnp.where(group == i, index[i], level)
    scales = jnp.full((1, ft), 0.125, F32)
    for i in range(1, 7):
        scales = jnp.where(level == i, 0.125 * 2**i, scales)
    loads[7].wait()
    TG[zh, y] = padded(th[...].astype(F32) * scales)

    def place(block, carry):
        row = lax.broadcasted_iota(jnp.int32, (ROWS, 16 * ROWS), 0)
        column = lax.broadcasted_iota(jnp.int32, (ROWS, 16 * ROWS), 1)
        source = jnp.full((ROWS, 16 * ROWS), -1, jnp.int32)
        for i in range(tokens):
            a = assign[block * tokens + i]
            source = jnp.where(row == i, lax.div(a, tokens) * ROWS + lax.rem(a, tokens), source)
        perm[block] = jnp.where(source == column, 1.0, 0.0).astype(BF)
        return carry

    loads[8].wait()
    lax.fori_loop(0, 16, place, 0)
    pl.semaphore_wait(barrier, len(partners))

    def columns(buf, z, low, high):
        return buf.at[z, y, :, pl.ds(low, high - low)]

    parts = ((XG, "Sz", "Sy", 0, xin.shape[1], 0), (TG, "Tz", "Ty", 0, ft, 0))
    for buf, nz, ny, low, high, slot in parts:
        own = columns(buf, zh, low, high)
        for k in KS:
            send(own, own, zh_dev(turn(zh, k)), nz, zh + slot)
    for buf, ny in ((XG, "Sy"), (TG, "Ty")):
        for k in KS:
            send(buf.at[zh, y], buf.at[zh, y], y_dev(turn(y, k)), ny, y)
    for buf, nz, ny, low, high, slot in parts:
        for k in KS:
            z = turn(zh, k)
            block = columns(buf, z, low, high)
            arrive(block, nz, z + slot)
            for j in KS:
                send(block, block, y_dev(turn(y, j)), ny, y)

    for j in KS:
        arrive(XG.at[:, turn(y, j)], "Sy", turn(y, j))
    loads[0].wait()
    loads[1].wait()
    half = XG[pl.ds(2 * oc, 2)].reshape(128, -1)
    for a, w in enumerate((wg, wu)):
        SCs[a] = dot(half, w[...]).reshape(SCs.shape[1:])
        send(SCs.at[a], SCr.at[a], core, "Sc", a)
    half = XG[pl.ds(2 * c, 2)].reshape(128, -1)
    for a, w in enumerate((wg, wu)):
        SOWN[a] = dot(half, w[...]).reshape(SOWN.shape[1:])

    for j in KS:
        arrive(TG.at[:, turn(y, j)], "Ty", turn(y, j))
    loads[2].wait()
    everything = TG[...].reshape(16 * ROWS, -1)
    picked = dot(perm[pl.ds(8 * oc, 8)].reshape(128, -1), everything).astype(BF)
    TCs[...] = dot(picked, td[...]).reshape(TCs.shape)
    for r in range(2):
        send(TCs.at[:, r], TCr.at[:, r], core, "Tc", r)
    picked = dot(perm[pl.ds(8 * c, 8)].reshape(128, -1), everything).astype(BF)
    TOWN[...] = dot(picked, td[...]).reshape(TOWN.shape)

    for a in range(2):
        arrive(SCr.at[a], "Sc", a)
        for k in KS:
            v = turn(x, k)
            SXs[v, a] = (SOWN[a, v] + SCr[a, v]).astype(BF)
            send(SXs.at[v, a], SXr.at[x, a], x_dev(v), "Sx", x * 2 + a)
    for r in range(2):
        scatter_x(TOWN, TCr, TXs, TXr, "Tc", "Tx", r)
    XT[...] = XG[...].reshape(16 * ROWS, -1).T

    fs = SOWN.shape[-1]
    shift = fs - 512
    for a in range(2):
        for k in KS:
            arrive(SXr.at[turn(x, k), a], "Sx", turn(x, k) * 2 + a)
        total = SOWN[a, x] + SCr[a, x]
        for k in KS:
            total = total + SXr[turn(x, k), a].astype(F32)
        for w in range(4):
            r, h = w % 2, w // 2
            part = total[r * 16 : r * 16 + 16, h * shift : h * shift + 512]
            SZf[w, a] = part
            SZs[w, a] = part.astype(BF)
        for k in KS:
            v = turn(zl, k)
            send(SZs.at[v, a], SZr.at[zl, a], zl_dev(v), "Szl", zl * 2 + a)
    piece = TZs.shape[-1]
    for r in range(2):
        total = TOWN[x, r] + TCr[x, r]
        for k in KS:
            arrive(TXr.at[turn(x, k), r], "Tx", turn(x, k) * 2 + r)
        for k in KS:
            total = total + TXr[turn(x, k), r]
        for w in range(4):
            TZs[w, r] = total[:, w * piece : (w + 1) * piece]
        for k in KS:
            v = turn(zl, k)
            send(TZs.at[v, r], TZr.at[zl, r], zl_dev(v), "Tzl", zl * 2 + r)

    pre = []
    for a in range(2):
        for k in KS:
            arrive(SZr.at[turn(zl, k), a], "Szl", turn(zl, k) * 2 + a)
        total = SZf[zl, a]
        for k in KS:
            total = total + SZr[turn(zl, k), a].astype(F32)
        pre.append(total)
    gate, up = pre
    sig = jax.nn.sigmoid(gate)
    HZ[zl] = (gate * sig * up).astype(BF)
    for k in KS:
        send(HZ.at[zl], HZ.at[zl], zl_dev(turn(zl, k)), "Hzl", zl)
    for r in range(2):
        total = TZs[zl, r]
        for k in KS:
            arrive(TZr.at[turn(zl, k), r], "Tzl", turn(zl, k) * 2 + r)
        for k in KS:
            total = total + TZr[turn(zl, k), r]
        TW[zl, r] = total.astype(BF)
        for k in KS:
            send(TW.at[zl, r], TW.at[zl, r], zl_dev(turn(zl, k)), "Tzg", zl * 2 + r)
    ABZ[zl, 0] = (up * sig * (1.0 + gate * (1.0 - sig))).astype(BF)
    ABZ[zl, 1] = (gate * sig).astype(BF)

    for k in KS:
        arrive(HZ.at[turn(zl, k)], "Hzl", turn(zl, k))
    for r in range(2):
        HID[c, x, r, :, 0:512] = HZ[r]
        HID[c, x, r, :, 512:fs] = HZ[2 + r][:, 512 - shift :]
    for k in KS:
        send(HID.at[c, x], HID.at[c, x], x_dev(turn(x, k)), "Hx", x)
    send(HID.at[c, x], HID.at[c, x], core, "Hc", 0)
    for r in range(2):
        for k in KS:
            arrive(TW.at[turn(zl, k), r], "Tzg", turn(zl, k) * 2 + r)
    AMd[zh, y] = jnp.full((8, 128), jnp.max(jnp.abs(TW[...].astype(F32))), F32)
    for p in dp_group:
        send(AMd.at[zh, y], AMd.at[zh, y], p, "Md", zh * 4 + y)
    for r in range(2):
        for w in range(4):
            TO[c, x, r, :, w * piece : (w + 1) * piece] = TW[w, r]
        mine = TO.at[c, x, r]
        for k in KS:
            send(mine, mine, x_dev(turn(x, k)), "Tax", x * 2 + r)
        send(mine, mine, core, "Tac", 0)

    for k in KS:
        v = turn(x, k)
        arrive(HID.at[c, v], "Hx", v)
        send(HID.at[c, v], HID.at[c, v], core, "Hc", 0)
    def product(rows, weights, full, rounded, half):
        out = dot(rows[half].reshape(8 * ROWS, -1), weights[...]).reshape(2, 4, ROWS, -1)
        full[pl.ds(2 * half, 2)] = out
        rounded[pl.ds(2 * half, 2)] = out.astype(BF)

    def spread(rounded, into, name):
        for k in KS:
            v = turn(y, k)
            send(rounded.at[:, v], into.at[y], y_dev(v), name, y)

    loads[4].wait()
    product(HID, wd, SPf, SPs, c)
    for r in range(2):
        pass_on(TO, "Tax", "Tac", r)
    arrive(HID.at[oc], "Hc", 0)
    product(HID, wd, SPf, SPs, oc)
    spread(SPs, SPr, "SPy")
    loads[3].wait()
    product(TO, dpj, TPf, TPs, c)
    arrive(TO.at[oc], "Tac", 0)
    product(TO, dpj, TPf, TPs, oc)
    spread(TPs, TPr, "TPy")

    for i in KS + (0,):
        for j in KS + (0,):
            if i or j:
                arrive(AMd.at[turn(zh, i), turn(y, j)], "Md", turn(zh, i) * 4 + turn(y, j))
    AMc[x, c] = jnp.max(AMd[...].reshape(16, 8, 128), axis=0)
    for p in pairs:
        send(AMc.at[x, c], AMc.at[x, c], p, "Mc", x * 2 + c)
    for k in KS:
        send(ABZ.at[zl], ABZ.at[zl], zl_dev(turn(zl, k)), "ABzl", zl)

    for k in KS:
        arrive(TPr.at[turn(y, k)], "TPy", turn(y, k))
        arrive(SPr.at[turn(y, k)], "SPy", turn(y, k))
    for k in KS:
        for b in range(2):
            arrive(AMc.at[turn(x, k), b], "Mc", turn(x, k) * 2 + b)
    arrive(AMc.at[x, oc], "Mc", x * 2 + oc)
    scale = (4.0 / jnp.max(AMc[...].reshape(8, 8, 128), axis=0))[0:1, 0:1]
    halves = (oc, c)
    for j, p in enumerate(halves):
        for i in range(2):
            z = 2 * p + i
            target, student = TPf[z, y], SPf[z, y]
            for k in KS:
                target = target + TPr[turn(y, k), z].astype(F32)
                student = student + SPr[turn(y, k), z].astype(F32)
            OZ[zh, z] = ((student - target * scale) * 0.5).astype(BF)
        part_of = OZ.at[zh, pl.ds(2 * p, 2)]
        for k in KS:
            send(part_of, part_of, zh_dev(turn(zh, k)), "Oz", zh * 2 + j)
    for k in KS:
        arrive(ABZ.at[turn(zl, k)], "ABzl", turn(zl, k))
    for a in range(2):
        for r in range(2):
            AB[c, x, a, r, :, 0:512] = ABZ[r, a]
            AB[c, x, a, r, :, 512:fs] = ABZ[2 + r, a][:, 512 - shift :]
    for k in KS:
        send(AB.at[c, x], AB.at[c, x], x_dev(turn(x, k)), "ABx", x)
    send(AB.at[c, x], AB.at[c, x], core, "ABc", 0)
    for j, p in enumerate(halves):
        for k in KS:
            arrive(OZ.at[turn(zh, k), pl.ds(2 * p, 2)], "Oz", turn(zh, k) * 2 + j)
        for i in range(2):
            z = 2 * p + i
            total = OZ[0, z].astype(F32)
            for w in range(1, 4):
                total = total + OZ[w, z].astype(F32)
            OG[z, y] = total.astype(BF)
        part_of = OG.at[pl.ds(2 * p, 2), y]
        for k in KS:
            send(part_of, part_of, y_dev(turn(y, k)), "Oy", y * 2 + j)

    for k in KS:
        v = turn(x, k)
        arrive(AB.at[c, v], "ABx", v)
        send(AB.at[c, v], AB.at[c, v], core, "ABc", 0)

    for k in KS:
        arrive(OG.at[pl.ds(2 * oc, 2), turn(y, k)], "Oy", turn(y, k) * 2)
    GCs[...] = dot_nt(OG[pl.ds(2 * oc, 2)].reshape(128, -1), wd[...]).astype(BF).reshape(GCs.shape)
    for r in range(2):
        send(GCs.at[:, r], GCr.at[:, r], core, "Gc", r)
    for k in KS:
        arrive(OG.at[pl.ds(2 * c, 2), turn(y, k)], "Oy", turn(y, k) * 2 + 1)
    GOWN[...] = dot_nt(OG[pl.ds(2 * c, 2)].reshape(128, -1), wd[...]).reshape(GOWN.shape)
    for r in range(2):
        scatter_x(GOWN, GCr, GXs, GXr, "Gc", "Gx", r)
    gd_o[...] = dot_tn(HID[...].reshape(16 * ROWS, -1), OG[...].reshape(16 * ROWS, -1)).astype(BF)
    store(gd_o, gd_h)
    for r in range(2):
        share_zl(GOWN, GCr, GXr, GZ, "Gx", "Gzl", r)
    for r in range(2):
        gather_x(GZ, HG, "Gzl", "Gax", "Gac", r)
    for r in range(2):
        pass_on(HG, "Gax", "Gac", r)

    def input_part(half):
        for v in range(4):
            g = HG[half, v].astype(F32)
            GG[half, v] = (g * AB[half, v, 0].astype(F32)).astype(BF)
            UG[half, v] = (g * AB[half, v, 1].astype(F32)).astype(BF)
        part = dot_nt(GG[half].reshape(8 * ROWS, -1), wg[...]) + dot_nt(UG[half].reshape(8 * ROWS, -1), wu[...])
        part = part.reshape(2, 4, ROWS, -1)
        IPf[pl.ds(2 * half, 2)] = part
        IPs[pl.ds(2 * half, 2)] = part.astype(BF)
        for i in range(2):
            z = 2 * half + i
            for k in KS:
                v = turn(y, k)
                send(IPs.at[z, v], IPr.at[y, z], y_dev(v), "Iy", y * 4 + z)

    input_part(c)
    arrive(AB.at[oc], "ABc", 0)
    arrive(HG.at[oc], "Gac", 0)
    input_part(oc)
    gates, ups = GG[...].reshape(16 * ROWS, -1), UG[...].reshape(16 * ROWS, -1)
    gg_o[...] = dot(XT[...], gates).astype(BF)
    store(gg_o, gg_h)
    for i in KS + (0,):
        z = turn(zh, i)
        for k in KS:
            arrive(IPr.at[turn(y, k), z], "Iy", turn(y, k) * 4 + z)
        total = IPf[z, y]
        for k in KS:
            total = total + IPr[turn(y, k), z].astype(F32)
        if i:
            IZs[z] = total.astype(BF)
            send(IZs.at[z], IZr.at[zh], zh_dev(z), "Iz", zh)
    gu_o[...] = dot(XT[...], ups).astype(BF)
    store(gu_o, gu_h)
    for k in KS:
        arrive(IZr.at[turn(zh, k)], "Iz", turn(zh, k))
    for k in KS:
        total = total + IZr[turn(zh, k)].astype(F32)
    ig_o[...] = total.astype(BF)
    store(ig_o, ig_h)
    for copy in sent[-N_SEND:]:
        copy.wait_send()
    for copy in stores:
        copy.wait()


def hand_over(gg, gu, gd, ig, gg_o, gu_o, gd_o, ig_o, gg_v, gu_v, gd_v, ig_v, sem):
    ways = []
    for a, b, o in ((gg, gg_v, gg_o), (gu, gu_v, gu_o), (gd, gd_v, gd_o)):
        part = a.shape[0] // 2
        ways += [tuple(r.at[pl.ds(i * part, part)] for r in (a, b, o)) for i in range(2)]
    loads = [pltpu.make_async_copy(a, b, sem.at[0, i]) for i, (a, b, _) in enumerate(ways)]
    stores = [pltpu.make_async_copy(b, o, sem.at[1, i]) for i, (_, b, o) in enumerate(ways)]
    last = pltpu.make_async_copy(ig, ig_v, sem.at[0, len(ways)])
    for load in loads + [last]:
        load.start()
    for load, store in zip(loads, stores):
        load.wait()
        store.start()
    last.wait()
    ig_o[...] = ig_v[...].astype(F32)[: ig_o.shape[0]].astype(BF)
    for store in stores:
        store.wait()


def body(
    teacher_hidden,
    teacher_down,
    scale_index,
    distill_proj,
    assignment,
    student_input,
    w_gate,
    w_up,
    w_down,
):
    tokens, ft = teacher_hidden.shape
    dt, ds = distill_proj.shape
    fs = w_gate.shape[1]

    def v(shape, dtype=BF):
        return pltpu.VMEM(shape, dtype)

    dp4 = (4, 4, ROWS)
    scratch = [
        pltpu.SMEM(scale_index.shape, jnp.int32), pltpu.SMEM(assignment.shape, jnp.int32), v((tokens, ft)), v((tokens, ds)),
        v((ds, fs)), v((ds, fs)), v((fs, ds)), v((ROWS, ds)),
        v((ft, dt)), v((dt, ds)), v((ds, fs)), v((ds, fs)), v((fs, ds)), v((16, ROWS, 16 * ROWS)), v(dp4 + (ft,)), v(dp4 + (ds,)), v((ds, 16 * ROWS)),
        v((2, 4, 32, fs), F32), v((2, 4, 32, fs), F32), v((2, 4, 32, fs), F32), v((4, 2, 32, fs)), v((4, 2, 32, fs)),
        v((4, 2, 16, 512), F32), v((4, 2, 16, 512)), v((4, 2, 16, 512)), v((4, 16, 512)), v((4, 2, 16, 512)),
        v((2, 4, 2, 16, fs)), v((2, 4, 2, 2, 16, fs)),
        v((4, 2, 16, dt), F32), v((4, 2, 16, dt), F32), v((4, 2, 16, dt), F32), v((4, 2, 16, dt), F32), v((4, 2, 16, dt), F32),
        v((4, 2, 16, dt // 4), F32), v((4, 2, 16, dt // 4), F32), v((4, 2, 16, dt // 4)), v((2, 4, 2, 16, dt)),
        v((4, 4, 8, 128), F32), v((4, 2, 8, 128), F32),
        v(dp4 + (ds,), F32), v(dp4 + (ds,)), v(dp4 + (ds,)), v(dp4 + (ds,), F32), v(dp4 + (ds,)), v(dp4 + (ds,)),
        v(dp4 + (ds,)), v(dp4 + (ds,)),
        v((4, 2, 16, fs)), v((4, 2, 16, fs)), v((4, 2, 16, fs), F32), v((4, 2, 16, fs)), v((4, 2, 16, fs)),
        v((4, 2, 16, fs)), v((2, 4, 2, 16, fs)), v((2, 4, 2, 16, fs)), v((2, 4, 2, 16, fs)),
        v(dp4 + (ds,), F32), v(dp4 + (ds,)), v(dp4 + (ds,)), v((4, ROWS, ds)), v((4, ROWS, ds)),
        pltpu.SemaphoreType.DMA((N_SEND,)), pltpu.SemaphoreType.DMA((N_RECV,)), pltpu.SemaphoreType.DMA((9,)), pltpu.SemaphoreType.DMA((4,)),
    ]
    vm, hbm = pl.BlockSpec(memory_space=pltpu.VMEM), pl.BlockSpec(memory_space=pl.ANY)
    sds = jax.ShapeDtypeStruct
    grad_gate, grad_up, grad_down, input_grad = pl.pallas_call(
        kernel,
        out_shape=(sds((ds, fs), BF), sds((ds, fs), BF), sds((fs, ds), BF), sds((ROWS, ds), BF)),
        in_specs=[hbm] * 9,
        out_specs=(hbm,) * 4,
        scratch_shapes=scratch,
        compiler_params=pltpu.CompilerParams(collective_id=0, has_side_effects=True, vmem_limit_bytes=56 << 20),
        name="distill_step",
    )(scale_index, assignment, teacher_hidden, student_input, teacher_down, distill_proj, w_gate, w_up, w_down)
    return pl.pallas_call(
        hand_over,
        out_shape=(sds((ds, fs), BF), sds((ds, fs), BF), sds((fs, ds), BF), sds((tokens, ds), BF)),
        in_specs=[hbm] * 4,
        out_specs=(hbm,) * 3 + (vm,),
        scratch_shapes=[v((ds, fs)), v((ds, fs)), v((fs, ds)), v((ROWS, ds)), pltpu.SemaphoreType.DMA((2, 7))],
        name="hand_over",
    )(grad_gate, grad_up, grad_down, input_grad)


def solution(mesh):
    placed = (
        P("dp", "mp"),
        P("mp", "dp"),
        P("mp"),
        P("dp", "mp"),
        P(),
        P("dp", "mp"),
        P("mp", "dp"),
        P("mp", "dp"),
        P("dp", "mp"),
    )
    return jax.shard_map(
        body,
        mesh=mesh,
        in_specs=placed,
        out_specs=(P("mp", "dp"), P("mp", "dp"), P("dp", "mp"), P("dp", "mp")),
        check_vma=False,
    )
```
